32 devices in a mesh: groups: 2 (over x), pb: 16 (over z, y, core).
Axes of the slice: x: 2, y: 2, z: 4, core: 2. Of those that a mesh axis runs over, the one named last changes fastest.
Arguments:
- tokens: bfloat16 [6144, 512], P(('groups', 'pb')), parts along dimension 0, may hold values from -6 to 6
- stamps: int32 [6144], P(('groups', 'pb')), parts along dimension 0, may hold values from 0 to 1086324736, as said below
- norm_gain: float32 [512], replicated, may hold values from 0.5 to 1.5
- w_proj: bfloat16 [512, 2048], replicated, may hold values from -0.25 to 0.25
- rel_bias: float32 [8, 16], replicated, may hold values from -1.5 to 1.5
- attn_gain: float32 [512], replicated, may hold values from 0.5 to 1.5
- w_out: bfloat16 [512, 512], replicated, may hold values from -0.25 to 0.25
Outputs:
- mixed: bfloat16 [6144, 512], P(('groups', 'pb')), parts along dimension 0
The draws below stay inside these ranges and needn't reach their ends.
There are 2 independent parts, one for each index of `groups`. The reference program is written for one: setup_inputs(seed, part) draws one part's arguments, and reference() takes and returns one part's arrays. A program takes and returns all parts, laid end to end along the dimension named above; an argument that names none is the same for every part. Nothing has to cross between parts.
Inputs may be any that keep to these rules, and one draw needn't show every extreme that they name: `stamps`: stamps never fall from one row to the next.
All inputs are finite; a program needn't handle non-finite values.
Results may differ from the reference program's by a relative error of at most 0.008.
Values may be sent and summed in bfloat16 or wider, within the bound.
No kernel may reach another device: no remote copies, remote signals or barrier semaphores. Data moves between devices by JAX's collectives and lax.ppermute only.
A program may use at most 128 MiB of HBM per device.

```python
import jax
import jax.numpy as jnp
from jax import lax

D = 512
HEADS = 8
HEAD = 64
BUCKETS = 16
TOK_DEV = 192
TOKENS = 3072


def draw_stamps(key, part):
    first_key = jax.random.fold_in(key, 11)
    second_key = jax.random.fold_in(key, 12)
    third_key = jax.random.fold_in(key, 13)
    exponent = jax.random.randint(first_key, (TOKENS,), 0, 13)
    chosen = jax.random.permutation(third_key, TOKENS)[:16]
    jump_bits = jnp.zeros((TOKENS,), jnp.int32).at[chosen].set(13 + jnp.arange(16, dtype=jnp.int32))
    jump_mask = jump_bits > 0
    exponent = jnp.where(jump_mask, jump_bits, exponent)
    ones_row = jnp.ones((TOKENS,), jnp.int32)
    low_end = jnp.where(jump_mask, jnp.left_shift(ones_row, exponent), 0)
    high_end = jnp.where(jump_mask, jnp.left_shift(ones_row, exponent + 1), jnp.left_shift(ones_row, exponent) + 1)
    spacing = jax.random.randint(second_key, (TOKENS,), low_end, high_end)
    running = jnp.cumsum(spacing).astype(jnp.int32)
    top_value = jnp.int32(4096 * TOKENS + 2 ** 30)
    return (running + (top_value - running[-1])).astype(jnp.int32)


def block_scale(key, extent, cuts, low, high):
    def one(position, blocks):
        draws = jax.random.uniform(jax.random.fold_in(jax.random.fold_in(key, 6), position), (blocks,), jnp.float32, low / len(cuts), high / len(cuts))
        return jnp.repeat(jnp.exp(draws), extent[position] // blocks).reshape((-1,) + (1,) * (len(extent) - position - 1))

    level = one(*cuts[0])
    for cut in cuts[1:]:
        level = level * one(*cut)
    return level


def gaussian(own_key, dims, scale, bound, cuts=(), kind=jnp.bfloat16):
    values = jax.random.normal(own_key, dims, jnp.float32) * scale
    if len(cuts) > 0:
        values = block_scale(own_key, dims, cuts, -0.22, 0.18) * values
    return jnp.clip(values, min=-bound, max=bound).astype(kind)


def setup_inputs(seed: int = 0, part: int = 0) -> dict:
    key_of = jax.random.split(jax.random.key(seed), 8)
    part_splits = jax.random.split(jax.random.fold_in(key_of[7], part), 8)
    return {
        "tokens": gaussian(part_splits[0], (TOKENS, D), 1.0, 6.0, ((0, 16),)),
        "stamps": draw_stamps(jax.random.fold_in(jax.random.fold_in(key_of[7], part), 71), part),
        "norm_gain": jnp.clip(1.0 + 0.1 * jax.random.normal(key_of[2], (D,), jnp.float32), 0.5, 1.5),
        "w_proj": gaussian(key_of[3], (D, 4 * D), D ** -0.5, 0.25),
        "rel_bias": jnp.clip(jax.random.uniform(key_of[4], (HEADS, BUCKETS), jnp.float32, -1.5, 1.5), -1.5, 1.5),
        "attn_gain": jnp.clip(1.0 + 0.1 * jax.random.normal(key_of[5], (D,), jnp.float32), 0.5, 1.5),
        "w_out": gaussian(key_of[6], (D, D), D ** -0.5, 0.25),
    }


epsilon = 1e-05

def layer_norm(values, gain):
    centered = values - lax.optimization_barrier(jnp.mean(values, axis=-1, keepdims=True))
    spread = lax.optimization_barrier(jnp.mean(centered * centered, axis=-1, keepdims=True))
    return centered * lax.rsqrt(spread + epsilon) * gain

def bucket_of(elapsed):
    bucket_ids = jnp.zeros(elapsed.shape, jnp.int32)
    for exponent in range(BUCKETS - 1):
        bucket_ids = bucket_ids + (elapsed >= 4 ** exponent).astype(jnp.int32)
    return bucket_ids

def reference(tokens, stamps, norm_gain, w_proj, rel_bias, attn_gain, w_out):
    normed = layer_norm(tokens.astype(jnp.float32), norm_gain).astype(jnp.bfloat16)
    projected = jnp.dot(normed, w_proj, preferred_element_type=jnp.float32)
    gate_vals = jax.nn.silu(projected[:, :D]).astype(jnp.bfloat16)
    queries = projected[:, D:2 * D].astype(jnp.bfloat16)
    key_rows = projected[:, 2 * D:3 * D].astype(jnp.bfloat16)
    value_rows = projected[:, 3 * D:].astype(jnp.bfloat16)
    q_heads = queries.astype(jnp.float32).reshape(TOKENS, HEADS, HEAD)
    k_heads = key_rows.astype(jnp.float32).reshape(TOKENS, HEADS, HEAD)
    v_heads = value_rows.astype(jnp.float32).reshape(TOKENS, HEADS, HEAD)
    positions = jnp.arange(TOKENS, dtype=jnp.int32)

    def one_block(start):
        q_block = lax.dynamic_slice_in_dim(q_heads, start, TOK_DEV, 0)
        q_pos = start + jnp.arange(TOK_DEV, dtype=jnp.int32)
        q_stamp = lax.dynamic_slice_in_dim(stamps, start, TOK_DEV, 0)
        scores = jnp.einsum('qhd,khd->hqk', q_block, k_heads) * HEAD ** (-0.5)
        bucket = bucket_of(q_stamp[:, None] - stamps[None, :])
        scores = scores + rel_bias[:, bucket]
        visible = positions[None, :] <= q_pos[:, None]
        weight = jnp.where(visible[None], jax.nn.silu(scores), 0.0).astype(jnp.bfloat16)
        mixture = jnp.einsum('hqk,khd->qhd', weight.astype(jnp.float32), v_heads)
        return mixture.reshape(TOK_DEV, D)
    block_starts = jnp.arange(0, TOKENS, TOK_DEV, dtype=jnp.int32)
    attended = lax.map(one_block, block_starts).reshape(TOKENS, D)
    gated = (layer_norm(attended, attn_gain) * gate_vals.astype(jnp.float32)).astype(jnp.bfloat16)
    result = tokens.astype(jnp.float32) + jnp.dot(gated, w_out, preferred_element_type=jnp.float32)
    return result.astype(jnp.bfloat16)
```

```python
import functools

import jax
import jax.numpy as jnp
from jax import lax
from jax.experimental import pallas as pl
from jax.experimental.pallas import tpu as pltpu
from jax.sharding import PartitionSpec as P

HEADS = 8
BUCKETS = 16
EPSILON = 1e-05
LANES = 128
TAIL = 16
HIDDEN = 64
BF16 = jnp.bfloat16
F32 = jnp.float32
I32 = jnp.int32
VMEM = pl.BlockSpec(memory_space=pltpu.VMEM)
SMEM = pl.BlockSpec(memory_space=pltpu.SMEM)


def layer_norm(values, gain):
    centered = values - jnp.mean(values, axis=-1, keepdims=True)
    spread = jnp.mean(centered * centered, axis=-1, keepdims=True)
    return centered * lax.rsqrt(spread + EPSILON) * gain


def call(kernel, outs, specs, args, flops, vmem=48 << 20):
    return pl.pallas_call(
        kernel,
        out_shape=outs,
        in_specs=specs,
        out_specs=jax.tree.map(lambda _: VMEM, outs),
        compiler_params=pltpu.CompilerParams(vmem_limit_bytes=vmem),
        cost_estimate=pl.CostEstimate(flops=flops, bytes_accessed=1 << 20, transcendentals=0),
    )(*args)


def norm_kernel(tokens_ref, stamps_ref, gain_ref, out_ref):
    rows, width = tokens_ref.shape
    out_ref[:rows, :] = layer_norm(tokens_ref[...].astype(F32), gain_ref[...]).astype(BF16)
    stamps = jnp.broadcast_to(stamps_ref[...], (TAIL, rows))
    byte = lax.broadcasted_iota(I32, (TAIL, rows), 0)
    part = jnp.where(byte < 4, lax.shift_right_logical(stamps, 8 * jnp.minimum(byte, 3)) & 255, 0)
    out_ref[rows:, :] = jnp.zeros((TAIL, width), BF16)
    out_ref[rows:, :rows] = part.astype(F32).astype(BF16)


def front_kernel(own_ref, stamps_ref, w_ref, bias_ref, q_ref, gate_ref, stamp_ref, table_ref):
    rows, width = q_ref.shape
    scale = 0.5 * (width // HEADS) ** -0.5
    normed = own_ref[:rows, :]
    gate = jnp.dot(normed, w_ref[:, :width], preferred_element_type=F32)
    gate_ref[...] = (gate / (1 + jnp.exp(-gate))).astype(BF16)
    queries = jnp.dot(normed, w_ref[:, width:], preferred_element_type=F32).astype(BF16)
    q_ref[...] = (queries.astype(F32) * scale).astype(BF16)
    pad = -rows % LANES
    stamps = jnp.concatenate([stamps_ref[...], jnp.zeros((1, pad), I32)], axis=1)
    stamp_ref[...] = jnp.broadcast_to(stamps, (LANES, rows + pad)).T[:rows, :]
    heads, buckets = bias_ref.shape
    bias = jnp.concatenate([bias_ref[...], jnp.zeros((heads, LANES - buckets), F32)], axis=1)
    lane = lax.broadcasted_iota(I32, (heads, LANES), 1)
    bucket = jnp.clip(lax.shift_right_logical(33 - jnp.minimum(lane, 32), 1), 0, buckets - 1)
    table = 0.5 * jnp.take_along_axis(bias, bucket, axis=1)
    table_ref[...] = jnp.where(lane < HIDDEN, table, -1e30)


def add_blocks(pos_ref, q_ref, stamp_ref, blocks, w_ref, table_ref, acc_ref):
    rows, width = q_ref.shape
    size = width // HEADS
    count = len(blocks)
    keys = count * rows
    normed = jnp.concatenate([b[:rows, :] for b in blocks], axis=0)
    key_rows = jnp.dot(normed, w_ref[:, :width], preferred_element_type=F32).astype(BF16)
    value_rows = jnp.dot(normed, w_ref[:, width:], preferred_element_type=F32).astype(BF16)
    stamps = []
    for b in blocks:
        part = b[rows : rows + TAIL, :rows].astype(F32).astype(I32)
        stamps.append(
            part[0:1] + part[1:2] * 256 + part[2:3] * 65536 + part[3:4] * 16777216
        )
    stamps = jnp.concatenate(stamps, axis=1)
    col = lax.broadcasted_iota(I32, (1, keys), 1)
    key_pos = pos_ref[1] + col
    for i in range(1, count):
        key_pos = jnp.where(col >= i * rows, pos_ref[1 + i] + col - i * rows, key_pos)
    row_pos = pos_ref[0] + lax.broadcasted_iota(I32, (rows, LANES), 0)
    index = []
    for j in range(keys // LANES):
        cut = slice(j * LANES, (j + 1) * LANES)
        elapsed = stamp_ref[...] - stamps[:, cut]
        index.append(jnp.where(key_pos[:, cut] <= row_pos, lax.clz(elapsed), HIDDEN))
    lane = lax.broadcasted_iota(I32, (1, LANES), 1)
    per = LANES // size
    for p in range(HEADS // per):
        cut = slice(p * LANES, (p + 1) * LANES)
        total = acc_ref[:, cut]
        for h in range(per):
            mine = (lane // size) == h
            q = jnp.where(mine, q_ref[:, cut], 0).astype(BF16)
            score = lax.dot_general(
                q, key_rows[:, cut], (((1,), (1,)), ((), ())), preferred_element_type=F32
            )
            head = p * per + h
            table = jnp.broadcast_to(table_ref[head : head + 1, :], (rows, LANES))
            bias = jnp.concatenate(
                [jnp.take_along_axis(table, i, axis=1) for i in index], axis=1
            )
            half = score + bias
            weight = (half * jnp.tanh(half) + half).astype(BF16)
            values = jnp.where(mine, value_rows[:, cut], 0).astype(BF16)
            total = total + jnp.dot(weight, values, preferred_element_type=F32)
        acc_ref[:, cut] = total


def attend_kernel(count, first, pos_ref, q_ref, stamp_ref, *refs):
    blocks, rest = refs[:count], refs[count:]
    if first:
        w_ref, table_ref, out_ref = rest
        out_ref[...] = jnp.zeros_like(out_ref)
    else:
        w_ref, table_ref, acc_ref, out_ref = rest
        out_ref[...] = acc_ref[...]

    @pl.when(pos_ref[1 + count] > 0)
    def _():
        add_blocks(pos_ref, q_ref, stamp_ref, blocks, w_ref, table_ref, out_ref)


def last_kernel(count, pos_ref, q_ref, stamp_ref, *refs):
    blocks, rest = refs[:count], refs[count:]
    w_ref, table_ref, acc_ref, gate_ref, gain_ref, wo_ref, tokens_ref, out_ref, sum_ref = rest
    sum_ref[...] = acc_ref[...]

    @pl.when(pos_ref[1 + count] > 0)
    def _():
        add_blocks(pos_ref, q_ref, stamp_ref, blocks, w_ref, table_ref, sum_ref)

    gated = layer_norm(sum_ref[...], gain_ref[...]) * gate_ref[...].astype(F32)
    mixed = jnp.dot(gated.astype(BF16), wo_ref[...], preferred_element_type=F32)
    out_ref[...] = (tokens_ref[...].astype(F32) + mixed).astype(BF16)


def body(shards, tokens, stamps, norm_gain, w_proj, rel_bias, attn_gain, w_out):
    me = lax.axis_index("pb")
    rows, width = tokens.shape
    near = 1
    while near < 4 and shards % (2 * near) == 0:
        near *= 2
    levels = shards // near
    flips = levels & (levels - 1) == 0
    stamps = stamps.reshape(1, rows)

    def swap(block, bit):
        return lax.ppermute(block, "pb", [(i, i ^ bit) for i in range(shards)])

    def far(block, step):
        if flips:
            return swap(block, step * near)
        return lax.ppermute(
            block, "pb", [(i, (i + step * near) % shards) for i in range(shards)]
        )

    def level_of(step):
        return (me // near) ^ step if flips else (me // near - step) % levels

    own = call(
        norm_kernel,
        jax.ShapeDtypeStruct((rows + TAIL, width), BF16),
        [VMEM] * 3,
        (tokens, stamps, norm_gain.reshape(1, width)),
        10 * rows * width,
    )
    groups = {}
    heads = [own] + [far(own, step) for step in range(levels - 1, 0, -1)]
    steps = [0] + list(range(levels - 1, 0, -1))
    for step, block in zip(steps, heads, strict=True):
        blocks = [(0, block)]
        bit = near // 2
        while bit:
            blocks = blocks + [(k ^ bit, swap(b, bit)) for k, b in blocks]
            bit //= 2
        groups[step] = blocks

    queries, gate, stamp_rows, table = call(
        front_kernel,
        (
            jax.ShapeDtypeStruct((rows, width), BF16),
            jax.ShapeDtypeStruct((rows, width), BF16),
            jax.ShapeDtypeStruct((rows, LANES), I32),
            jax.ShapeDtypeStruct((rel_bias.shape[0], LANES), F32),
        ),
        [VMEM] * 4,
        (own, stamps, w_proj[:, : 2 * width], rel_bias),
        4 * rows * width * width,
    )
    back = w_proj[:, 2 * width :]
    total = None
    for step in steps:
        blocks = groups[step]
        level = level_of(step)
        pos = jnp.stack(
            [me * rows]
            + [(level * near + ((me % near) ^ k)) * rows for k, _ in blocks]
            + [(level <= me // near).astype(I32)]
        ).astype(I32)
        count = len(blocks)
        specs = [SMEM] + [VMEM] * (4 + count)
        args = [pos, queries, stamp_rows, *(b for _, b in blocks), back, table]
        flops = 8 * count * rows * width * (width + rows)
        if total is not None:
            args.append(total)
            specs.append(VMEM)
        if step != steps[-1]:
            total = call(
                functools.partial(attend_kernel, count, total is None),
                jax.ShapeDtypeStruct((rows, width), F32),
                specs,
                args,
                flops,
            )
            continue
        args += [gate, attn_gain.reshape(1, width), w_out, tokens]
        return pl.pallas_call(
            functools.partial(last_kernel, count),
            out_shape=jax.ShapeDtypeStruct((rows, width), BF16),
            in_specs=specs + [VMEM] * 4,
            out_specs=VMEM,
            scratch_shapes=[pltpu.VMEM((rows, width), F32)],
            compiler_params=pltpu.CompilerParams(vmem_limit_bytes=48 << 20),
        )(*args)


def solution(mesh):
    return jax.shard_map(
        functools.partial(body, mesh.shape["pb"]),
        mesh=mesh,
        in_specs=(P(("groups", "pb"), None), P(("groups", "pb")), P(), P(), P(), P(), P()),
        out_specs=P(("groups", "pb"), None),
        check_vma=False,
    )
```

```python
import functools

import jax
import jax.numpy as jnp
from jax import lax
from jax.experimental import pallas as pl
from jax.experimental.pallas import tpu as pltpu
from jax.sharding import PartitionSpec as P

HEADS = 8
BUCKETS = 16
EPSILON = 1e-05
LANES = 128
TAIL = 16
HIDDEN = 64
BF16 = jnp.bfloat16
F32 = jnp.float32
I32 = jnp.int32
VMEM = pl.BlockSpec(memory_space=pltpu.VMEM)
SMEM = pl.BlockSpec(memory_space=pltpu.SMEM)
HBM = pl.BlockSpec(memory_space=pltpu.HBM)
VMEM_LIMIT = 12 << 20


def layer_norm(values, gain):
    centered = values - jnp.mean(values, axis=-1, keepdims=True)
    spread = jnp.mean(centered * centered, axis=-1, keepdims=True)
    return centered * lax.rsqrt(spread + EPSILON) * gain


def norm_kernel(tokens_hbm, stamps_hbm, gain_hbm, out_ref, tokens_ref, stamps_ref, gain_ref, sems):
    copies = [
        pltpu.make_async_copy(src, dst, sems.at[i])
        for i, (src, dst) in enumerate(
            ((tokens_hbm, tokens_ref), (stamps_hbm, stamps_ref), (gain_hbm, gain_ref))
        )
    ]
    for copy in copies:
        copy.start()
    for copy in copies:
        copy.wait()
    rows, width = tokens_ref.shape
    out_ref[:rows, :] = layer_norm(tokens_ref[...].astype(F32), gain_ref[...]).astype(BF16)
    stamps = jnp.broadcast_to(stamps_ref[...], (TAIL, rows))
    byte = lax.broadcasted_iota(I32, (TAIL, rows), 0)
    part = jnp.where(byte < 4, lax.shift_right_logical(stamps, 8 * jnp.minimum(byte, 3)) & 255, 0)
    out_ref[rows:, :] = jnp.zeros((TAIL, width), BF16)
    out_ref[rows:, :rows] = part.astype(F32).astype(BF16)


def stamps_of(block):
    rows = block.shape[0] - TAIL
    part = block[rows:, :rows].astype(F32).astype(I32)
    return part[0:1] + part[1:2] * 256 + part[2:3] * 65536 + part[3:4] * 16777216


def down_rows(stamps):
    rows = stamps.shape[1]
    pad = -rows % LANES
    stamps = jnp.concatenate([stamps, jnp.zeros((1, pad), I32)], axis=1)
    return jnp.broadcast_to(stamps, (LANES, rows + pad)).T[:rows, :]


def queries_of(normed, weight):
    width = normed.shape[1]
    scale = 0.5 * (width // HEADS) ** -0.5
    queries = jnp.dot(normed, weight, preferred_element_type=F32)
    return (queries.astype(BF16).astype(F32) * scale).astype(BF16)


def relay_kernel(own_ref, other_ref, out_ref):
    del other_ref
    out_ref[...] = own_ref[...]


def front_kernel(own_ref, w_ref, bias_ref, q_ref, gate_ref, stamp_ref, table_ref):
    rows, width = q_ref.shape
    stamp_ref[...] = down_rows(stamps_of(own_ref))
    normed = own_ref[:rows, :]
    gate = jnp.dot(normed, w_ref[:, :width], preferred_element_type=F32)
    gate_ref[...] = (gate / (1 + jnp.exp(-gate))).astype(BF16)
    q_ref[...] = queries_of(normed, w_ref[:, width : 2 * width])
    heads, buckets = bias_ref.shape
    bias = jnp.concatenate([bias_ref[...], jnp.zeros((heads, LANES - buckets), F32)], axis=1)
    lane = lax.broadcasted_iota(I32, (heads, LANES), 1)
    bucket = jnp.clip(lax.shift_right_logical(33 - jnp.minimum(lane, 32), 1), 0, buckets - 1)
    table = 0.5 * jnp.take_along_axis(bias, bucket, axis=1)
    table_ref[...] = jnp.where(lane < HIDDEN, table, -1e30)


def add_blocks(first_row, first_keys, q_ref, stamp_ref, blocks, w_ref, table_ref, acc_ref):
    rows, width = q_ref.shape
    size = width // HEADS
    count = len(blocks)
    keys = count * rows
    normed = jnp.concatenate([b[:rows, :] for b in blocks], axis=0)
    key_rows = jnp.dot(normed, w_ref[:, 2 * width : 3 * width], preferred_element_type=F32).astype(BF16)
    value_rows = jnp.dot(normed, w_ref[:, 3 * width :], preferred_element_type=F32).astype(BF16)
    stamps = jnp.concatenate([stamps_of(b) for b in blocks], axis=1)
    col = lax.broadcasted_iota(I32, (1, keys), 1)
    key_pos = first_keys[0] + col
    for i in range(1, count):
        key_pos = jnp.where(col >= i * rows, first_keys[i] + col - i * rows, key_pos)
    row_pos = first_row + lax.broadcasted_iota(I32, (rows, LANES), 0)
    index = []
    for j in range(keys // LANES):
        cut = slice(j * LANES, (j + 1) * LANES)
        elapsed = stamp_ref[...] - stamps[:, cut]
        index.append(jnp.where(key_pos[:, cut] <= row_pos, lax.clz(elapsed), HIDDEN))
    lane = lax.broadcasted_iota(I32, (1, LANES), 1)
    per = LANES // size
    for p in range(HEADS // per):
        cut = slice(p * LANES, (p + 1) * LANES)
        total = acc_ref[:, cut]
        for h in range(per):
            mine = (lane // size) == h
            q = jnp.where(mine, q_ref[:, cut], 0).astype(BF16)
            score = lax.dot_general(
                q, key_rows[:, cut], (((1,), (1,)), ((), ())), preferred_element_type=F32
            )
            head = p * per + h
            table = jnp.broadcast_to(table_ref[head : head + 1, :], (rows, LANES))
            bias = jnp.concatenate(
                [jnp.take_along_axis(table, i, axis=1) for i in index], axis=1
            )
            half = score + bias
            weight = (half * jnp.tanh(half) + half).astype(BF16)
            values = jnp.where(mine, value_rows[:, cut], 0).astype(BF16)
            total = total + jnp.dot(weight, values, preferred_element_type=F32)
        acc_ref[:, cut] = total


def add_sets(sizes, pos_ref, q_ref, stamp_ref, blocks, w_ref, table_ref, acc_ref):
    at, done = 1, 0
    for size in sizes:
        keys = [pos_ref[at + 1 + i] for i in range(size)]
        part = blocks[done : done + size]

        @pl.when(pos_ref[at] > 0)
        def _(keys=keys, part=part):
            add_blocks(pos_ref[0], keys, q_ref, stamp_ref, part, w_ref, table_ref, acc_ref)

        at, done = at + 1 + size, done + size


def attend_kernel(sizes, first, pos_ref, q_ref, stamp_ref, *refs):
    count = sum(sizes)
    blocks, rest = refs[:count], refs[count:]
    if first:
        w_ref, table_ref, out_ref, tick_ref = rest
        out_ref[...] = jnp.zeros_like(out_ref)
    else:
        w_ref, table_ref, acc_ref, _, out_ref, tick_ref = rest
        out_ref[...] = acc_ref[...]
    add_sets(sizes, pos_ref, q_ref, stamp_ref, blocks, w_ref, table_ref, out_ref)
    tick_ref[...] = jnp.zeros_like(tick_ref)


def return_kernel(count, pos_ref, asked_ref, *refs):
    blocks, rest = refs[:count], refs[count:]
    w_ref, table_ref, out_ref, tick_ref, q_ref, stamp_ref, sum_ref = rest
    tick_ref[...] = jnp.zeros_like(tick_ref)

    @pl.when(pos_ref[1] > 0)
    def _():
        rows = out_ref.shape[0]
        q_ref[...] = queries_of(asked_ref[:rows, :], w_ref[:, w_ref.shape[1] // 4 : w_ref.shape[1] // 2])
        stamp_ref[...] = down_rows(stamps_of(asked_ref))
        sum_ref[...] = jnp.zeros_like(sum_ref)
        add_sets((count,), pos_ref, q_ref, stamp_ref, blocks, w_ref, table_ref, sum_ref)
        out_ref[...] = sum_ref[...].astype(BF16)


def last_kernel(sum_ref, given_ref, gate_ref, gain_ref, wo_ref, tokens_ref, out_ref):
    attended = sum_ref[...] + given_ref[...].astype(F32)
    gated = layer_norm(attended, gain_ref[...]) * gate_ref[...].astype(F32)
    mixed = jnp.dot(gated.astype(BF16), wo_ref[...], preferred_element_type=F32)
    out_ref[...] = (tokens_ref[...].astype(F32) + mixed).astype(BF16)


def pin_kernel(block_ref, tick_ref, out_ref):
    del block_ref, tick_ref, out_ref


def pin(block, tick):
    return pl.pallas_call(
        pin_kernel,
        out_shape=jax.ShapeDtypeStruct(block.shape, block.dtype),
        in_specs=[pl.BlockSpec(memory_space=pl.ANY)] * 2,
        out_specs=pl.BlockSpec(memory_space=pl.ANY),
        input_output_aliases={0: 0},
        compiler_params=pltpu.CompilerParams(vmem_limit_bytes=1 << 20),
    )(block, tick)


def body(shards, tokens, stamps, norm_gain, w_proj, rel_bias, attn_gain, w_out):
    me = lax.axis_index("pb")
    rows, width = tokens.shape
    near = 4
    levels = shards // near
    level, spot = me // near, me % near

    def swap(block, bit):
        return lax.ppermute(block, "pb", [(i, i ^ bit) for i in range(shards)])

    def hop(block, pairs):
        return lax.ppermute(
            block, "pb", [(a * near + i, b * near + i) for a, b in pairs for i in range(near)]
        )

    own = pl.pallas_call(
        norm_kernel,
        out_shape=jax.ShapeDtypeStruct((rows + TAIL, width), BF16),
        in_specs=[HBM] * 3,
        out_specs=VMEM,
        scratch_shapes=[
            pltpu.VMEM((rows, width), BF16),
            pltpu.VMEM((1, rows), I32),
            pltpu.VMEM((1, width), F32),
            pltpu.SemaphoreType.DMA((3,)),
        ],
        compiler_params=pltpu.CompilerParams(vmem_limit_bytes=56 << 20),
    )(tokens, stamps.reshape(1, rows), norm_gain.reshape(1, width))

    far = {}
    for step in range(levels - 2, 0, -1):
        pairs = [(z, z + step) for z in range(levels - step)]
        if step == levels - 2:
            pairs.append((levels - 1, 0))
        far[step] = hop(own, pairs)
    by_core = swap(own, 1)
    own = pl.pallas_call(
        relay_kernel,
        out_shape=jax.ShapeDtypeStruct(own.shape, BF16),
        in_specs=[VMEM] * 2,
        out_specs=VMEM,
        compiler_params=pltpu.CompilerParams(vmem_limit_bytes=2 << 20),
    )(own, by_core)
    by_y = swap(own, 2)
    queries, gate, stamp_rows, table = pl.pallas_call(
        front_kernel,
        out_shape=(
            jax.ShapeDtypeStruct((rows, width), BF16),
            jax.ShapeDtypeStruct((rows, width), BF16),
            jax.ShapeDtypeStruct((rows, LANES), I32),
            jax.ShapeDtypeStruct((rel_bias.shape[0], LANES), F32),
        ),
        in_specs=[VMEM] * 3,
        out_specs=(VMEM,) * 4,
        compiler_params=pltpu.CompilerParams(vmem_limit_bytes=VMEM_LIMIT),
        cost_estimate=pl.CostEstimate(
            flops=4 * rows * width * width, bytes_accessed=5 << 18, transcendentals=0
        ),
    )(own, w_proj, rel_bias)

    def row_of(step, bits):
        return ((level - step) * near + (spot ^ bits)) * rows

    def positions(sets):
        pos = [me * rows]
        for step, blocks in sets:
            seen = [row_of(step, bits) for bits, _ in blocks]
            flag = functools.reduce(jnp.minimum, seen) <= me * rows
            pos += [(flag & (level >= step)).astype(I32), *seen]
        return jnp.stack(pos).astype(I32)

    tick_shape = jax.ShapeDtypeStruct((8, LANES), F32)

    def attend(sets, total, *more, weight=8):
        sizes = tuple(len(blocks) for _, blocks in sets)
        blocks = [b for _, part in sets for _, b in part]
        args = [positions(sets), queries, stamp_rows, *blocks, w_proj, table]
        args += [] if total is None else [total]
        args += more
        flops = weight * len(blocks) * rows * width * (width + rows)
        return pl.pallas_call(
            functools.partial(attend_kernel, sizes, total is None),
            out_shape=(jax.ShapeDtypeStruct((rows, width), F32), tick_shape),
            in_specs=[SMEM] + [VMEM] * (len(args) - 1),
            out_specs=(VMEM, VMEM),
            compiler_params=pltpu.CompilerParams(vmem_limit_bytes=VMEM_LIMIT),
            cost_estimate=pl.CostEstimate(
                flops=flops, bytes_accessed=weight << 17, transcendentals=0
            ),
        )(*args)

    total, tick = attend([(0, [(0, own), (1, by_core)])], None)
    by_y = pin(by_y, tick)
    by_both = swap(by_y, 1)
    total, tick = attend([(0, [(2, by_y), (3, by_both)])], total, tick)
    here = [(0, own), (1, by_core), (2, by_y), (3, by_both)]
    across = {}
    for step in sorted(far):
        block = far[step]
        if step == levels - 2:
            block = far[step] = pin(block, tick)
        across[step] = swap(block, 2)
        beside = swap(block, 1)
        if step == levels - 2:
            pos = jnp.stack(
                [((levels - 1) * near + spot) * rows, (level == 0).astype(I32)]
                + [(spot ^ bits) * rows for bits, _ in here]
            ).astype(I32)
            returned, tick = pl.pallas_call(
                functools.partial(return_kernel, near),
                out_shape=(jax.ShapeDtypeStruct((rows, width), BF16), tick_shape),
                in_specs=[SMEM] + [VMEM] * (near + 3),
                out_specs=(VMEM, VMEM),
                scratch_shapes=[
                    pltpu.VMEM((rows, width), BF16),
                    pltpu.VMEM((rows, LANES), I32),
                    pltpu.VMEM((rows, width), F32),
                ],
                compiler_params=pltpu.CompilerParams(vmem_limit_bytes=VMEM_LIMIT),
                cost_estimate=pl.CostEstimate(
                    flops=32 * rows * width * (width + rows),
                    bytes_accessed=1 << 20,
                    transcendentals=0,
                ),
            )(pos, block, *(b for _, b in here), w_proj, table)
            given = hop(returned, [(0, levels - 1)])
        far[step] = [(0, block), (1, beside)]
    ticks = []
    for step in sorted(far):
        total, tick = attend([(step, far[step])], total, tick)
        ticks.append(tick)
    for step, done in zip(sorted(far), ticks, strict=True):
        block = pin(across[step], done)
        sets = [(step, [(2, block), (3, swap(block, 1))])]
        total, tick = attend(sets, total, tick, weight=1)
    return pl.pallas_call(
        last_kernel,
        out_shape=jax.ShapeDtypeStruct((rows, width), BF16),
        in_specs=[VMEM] * 6,
        out_specs=VMEM,
        compiler_params=pltpu.CompilerParams(vmem_limit_bytes=VMEM_LIMIT),
    )(total, given, gate, attn_gain.reshape(1, width), w_out, tokens)


def solution(mesh):
    return jax.shard_map(
        functools.partial(body, mesh.shape["pb"]),
        mesh=mesh,
        in_specs=(P(("groups", "pb"), None), P(("groups", "pb")), P(), P(), P(), P(), P()),
        out_specs=P(("groups", "pb"), None),
        check_vma=False,
    )
```

```python
import functools

import jax
import jax.numpy as jnp
from jax import lax
from jax.experimental import pallas as pl
from jax.experimental.pallas import tpu as pltpu
from jax.sharding import PartitionSpec as P

HEADS = 8
BUCKETS = 16
EPSILON = 1e-05
LANES = 128
TAIL = 16
COST = (4, 16, 16, 32, 32, 1, 0)
FIXED = 15
BF16 = jnp.bfloat16
F32 = jnp.float32
I32 = jnp.int32
VMEM = pl.BlockSpec(memory_space=pltpu.VMEM)
SMEM = pl.BlockSpec(memory_space=pltpu.SMEM)
HBM = pl.BlockSpec(memory_space=pltpu.HBM)
VMEM_LIMIT = 12 << 20


def layer_norm(values, gain):
    centered = values - jnp.mean(values, axis=-1, keepdims=True)
    spread = jnp.mean(centered * centered, axis=-1, keepdims=True)
    return centered * lax.rsqrt(spread + EPSILON) * gain


def norm_kernel(tokens_hbm, stamps_hbm, gain_hbm, out_ref, tokens_ref, stamps_ref, gain_ref, sems):
    copies = [
        pltpu.make_async_copy(src, dst, sems.at[i])
        for i, (src, dst) in enumerate(
            ((tokens_hbm, tokens_ref), (stamps_hbm, stamps_ref), (gain_hbm, gain_ref))
        )
    ]
    for copy in copies:
        copy.start()
    for copy in copies:
        copy.wait()
    rows, width = tokens_ref.shape
    out_ref[:rows, :] = layer_norm(tokens_ref[...].astype(F32), gain_ref[...]).astype(BF16)
    stamps = jnp.broadcast_to(stamps_ref[...], (TAIL, rows))
    byte = lax.broadcasted_iota(I32, (TAIL, rows), 0)
    part = jnp.where(byte < 4, lax.shift_right_logical(stamps, 8 * jnp.minimum(byte, 3)) & 255, 0)
    out_ref[rows:, :] = jnp.zeros((TAIL, width), BF16)
    out_ref[rows:, :rows] = part.astype(F32).astype(BF16)


def stamps_of(block):
    rows = block.shape[0] - TAIL
    part = block[rows:, :rows].astype(F32).astype(I32)
    return part[0:1] + part[1:2] * 256 + part[2:3] * 65536 + part[3:4] * 16777216


def down_rows(stamps):
    rows = stamps.shape[1]
    pad = -rows % LANES
    stamps = jnp.concatenate([stamps, jnp.zeros((1, pad), I32)], axis=1)
    return jnp.broadcast_to(stamps, (LANES, rows + pad)).T[:rows, :]


def queries_of(normed, weight):
    width = normed.shape[1]
    scale = 0.5 * (width // HEADS) ** -0.5
    queries = jnp.dot(normed, weight, preferred_element_type=F32)
    return (queries.astype(BF16).astype(F32) * scale).astype(BF16)


def relay_kernel(own_ref, other_ref, out_ref):
    del other_ref
    out_ref[...] = own_ref[...]


def front_kernel(own_ref, w_ref, bias_ref, q_ref, gate_ref, stamp_ref, table_ref):
    rows, width = q_ref.shape
    stamp_ref[...] = down_rows(stamps_of(own_ref))
    normed = own_ref[:rows, :]
    gate = jnp.dot(normed, w_ref[:, :width], preferred_element_type=F32)
    gate_ref[...] = (gate / (1 + jnp.exp(-gate))).astype(BF16)
    q_ref[...] = queries_of(normed, w_ref[:, width : 2 * width])
    heads, buckets = bias_ref.shape
    bias = jnp.concatenate([bias_ref[...], jnp.zeros((heads, LANES - buckets), F32)], axis=1)
    lane = lax.broadcasted_iota(I32, (heads, LANES), 1)
    bucket = jnp.clip(lax.shift_right_logical(33 - jnp.minimum(lane, 32), 1), 0, buckets - 1)
    half = 0.5 * jnp.take_along_axis(bias, bucket, axis=1)
    for p in range(heads // 2):
        low = jnp.floor(half[2 * p + 1 : 2 * p + 2] * 2.0**FIXED + 0.5)
        high = jnp.floor(half[2 * p : 2 * p + 1] * 2.0**FIXED - low * 2.0**-16 + 0.5)
        table_ref[p : p + 1, :] = high.astype(I32) * 65536 + low.astype(I32)


def add_blocks(q_ref, stamp_ref, blocks, w_ref, table_ref, acc_ref, out_ref, hide=None, more_ref=None):
    rows, width = q_ref.shape
    size = width // HEADS
    keys = len(blocks) * rows
    normed = jnp.concatenate([b[:rows, :] for b in blocks], axis=0)
    key_rows = jnp.dot(
        normed, w_ref[:, 2 * width : 3 * width], preferred_element_type=F32
    ).astype(BF16)
    value_rows = jnp.dot(normed, w_ref[:, 3 * width :], preferred_element_type=F32).astype(BF16)
    stamps = jnp.concatenate([stamps_of(b) for b in blocks], axis=1)
    cuts = [slice(j * LANES, (j + 1) * LANES) for j in range(keys // LANES)]
    index = [lax.clz(stamp_ref[...] - stamps[:, cut]) for cut in cuts]
    head = lax.broadcasted_iota(I32, (1, LANES), 1) // size
    zero = jnp.zeros((), BF16)
    for p in range(HEADS // 2):
        pair = slice(p * LANES, (p + 1) * LANES)
        both = jnp.concatenate(
            [jnp.where(head == h, key_rows[:, pair], zero) for h in (0, 1)], axis=0
        )
        score = lax.dot_general(
            q_ref[:, pair], both, (((1,), (1,)), ((), ())), preferred_element_type=F32
        )
        table = jnp.broadcast_to(table_ref[p : p + 1, :], (rows, LANES))
        words = [jnp.take_along_axis(table, i, axis=1) for i in index]
        weight = []
        for h in (0, 1):
            for j, word in enumerate(words):
                code = lax.shift_left(word, 16) if h else word
                at = h * keys + j * LANES
                half = score[:, at : at + LANES] + code.astype(F32) * 2.0 ** (-16 - FIXED)
                if hide is not None:
                    half = half + hide[j]
                weight.append((half * jnp.tanh(half) + half).astype(BF16))
        values = jnp.concatenate(
            [jnp.where(head == h, value_rows[:, pair], zero) for h in (0, 1)], axis=0
        )
        mixed = jnp.dot(
            jnp.concatenate(weight, axis=1), values, preferred_element_type=F32
        )
        if acc_ref is not None:
            mixed = acc_ref[:, pair] + mixed
        if more_ref is not None:
            mixed = more_ref[:, pair].astype(F32) + mixed
        out_ref[:, pair] = mixed.astype(out_ref.dtype)


def place(near):
    me = lax.axis_index("pb")
    return me // near, me % near


def own_kernel(q_ref, stamp_ref, own_ref, other_ref, w_ref, table_ref, out_ref, tick_ref):
    rows = q_ref.shape[0]
    core = lax.axis_index("pb") % 2
    col = lax.broadcasted_iota(I32, (1, 2 * rows), 1)
    key = jnp.where(col < rows, core * rows + col, (1 - core) * rows + col - rows)
    query = core * rows + lax.broadcasted_iota(I32, (rows, LANES), 0)
    hide = [
        jnp.where(key[:, at : at + LANES] <= query, 0.0, -1e30)
        for at in range(0, 2 * rows, LANES)
    ]
    blocks = (own_ref, other_ref)
    add_blocks(q_ref, stamp_ref, blocks, w_ref, table_ref, None, out_ref, hide)
    tick_ref[...] = jnp.zeros_like(tick_ref)


def attend_kernel(near, step, given, tell, q_ref, stamp_ref, *refs):
    blocks = refs[:2]
    w_ref, table_ref, acc_ref = refs[2:5]
    out_ref = refs[-2] if tell else refs[-1]
    more_ref = refs[5] if given else None
    level, spot = place(near)
    seen = level >= step if step else spot >= near // 2

    @pl.when(seen)
    def _():
        add_blocks(
            q_ref, stamp_ref, blocks, w_ref, table_ref, acc_ref, out_ref, more_ref=more_ref
        )

    @pl.when(jnp.logical_not(seen))
    def _():
        kept = acc_ref[...]
        out_ref[...] = kept + more_ref[...].astype(F32) if given else kept

    if tell:
        refs[-1][...] = jnp.zeros_like(refs[-1])


def return_kernel(near, asked_ref, *refs):
    blocks = refs[:near]
    w_ref, table_ref, out_ref, tick_ref, q_ref, stamp_ref = refs[near:]
    tick_ref[...] = jnp.zeros_like(tick_ref)

    @pl.when(place(near)[0] == 0)
    def _():
        rows, width = out_ref.shape
        q_ref[...] = queries_of(asked_ref[:rows, :], w_ref[:, width : 2 * width])
        stamp_ref[...] = down_rows(stamps_of(asked_ref))
        add_blocks(q_ref, stamp_ref, blocks, w_ref, table_ref, None, out_ref)


def last_kernel(near, steps, q_ref, stamp_ref, *refs):
    count = 2 * len(steps)
    blocks = refs[:count]
    w_ref, table_ref, acc_ref, gate_ref, gain_ref, wo_ref, tokens_ref = refs[count:-2]
    out_ref, sum_ref = refs[-2:]
    level = place(near)[0]
    for i in range(len(steps) + 1):
        low = level >= steps[i - 1] if i else True
        high = level < steps[i] if i < len(steps) else True

        @pl.when(jnp.logical_and(low, high))
        def _(i=i):
            if i == 0:
                sum_ref[...] = acc_ref[...]
            else:
                seen = blocks[: 2 * i]
                add_blocks(q_ref, stamp_ref, seen, w_ref, table_ref, acc_ref, sum_ref)

    gated = layer_norm(sum_ref[...], gain_ref[...]) * gate_ref[...].astype(F32)
    mixed = jnp.dot(gated.astype(BF16), wo_ref[...], preferred_element_type=F32)
    out_ref[...] = (tokens_ref[...].astype(F32) + mixed).astype(BF16)


def pin_kernel(block_ref, tick_ref, out_ref):
    del block_ref, tick_ref, out_ref


def pin(block, tick):
    return pl.pallas_call(
        pin_kernel,
        out_shape=jax.ShapeDtypeStruct(block.shape, block.dtype),
        in_specs=[pl.BlockSpec(memory_space=pl.ANY)] * 2,
        out_specs=pl.BlockSpec(memory_space=pl.ANY),
        input_output_aliases={0: 0},
        compiler_params=pltpu.CompilerParams(vmem_limit_bytes=1 << 20),
    )(block, tick)


def body(shards, tokens, stamps, norm_gain, w_proj, rel_bias, attn_gain, w_out):
    rows, width = tokens.shape
    near = 4
    levels = shards // near

    def swap(block, bit):
        return lax.ppermute(block, "pb", [(i, i ^ bit) for i in range(shards)])

    def hop(block, pairs):
        return lax.ppermute(
            block, "pb", [(a * near + i, b * near + i) for a, b in pairs for i in range(near)]
        )

    own = pl.pallas_call(
        norm_kernel,
        out_shape=jax.ShapeDtypeStruct((rows + TAIL, width), BF16),
        in_specs=[HBM] * 3,
        out_specs=VMEM,
        scratch_shapes=[
            pltpu.VMEM((rows, width), BF16),
            pltpu.VMEM((1, rows), I32),
            pltpu.VMEM((1, width), F32),
            pltpu.SemaphoreType.DMA((3,)),
        ],
        compiler_params=pltpu.CompilerParams(vmem_limit_bytes=56 << 20),
    )(tokens, stamps.reshape(1, rows), norm_gain.reshape(1, width))

    far = {}
    for step in range(levels - 2, 0, -1):
        pairs = [(z, z + step) for z in range(levels - step)]
        if step == levels - 2:
            pairs.append((levels - 1, 0))
        far[step] = hop(own, pairs)
    by_core = swap(own, 1)
    own = pl.pallas_call(
        relay_kernel,
        out_shape=jax.ShapeDtypeStruct(own.shape, BF16),
        in_specs=[VMEM] * 2,
        out_specs=VMEM,
        compiler_params=pltpu.CompilerParams(vmem_limit_bytes=2 << 20),
        cost_estimate=pl.CostEstimate(
            flops=COST[6] * rows * width * width, bytes_accessed=0, transcendentals=0
        ),
    )(own, by_core)
    by_y = swap(own, 2)
    queries, gate, stamp_rows, table = pl.pallas_call(
        front_kernel,
        out_shape=(
            jax.ShapeDtypeStruct((rows, width), BF16),
            jax.ShapeDtypeStruct((rows, width), BF16),
            jax.ShapeDtypeStruct((rows, LANES), I32),
            jax.ShapeDtypeStruct((rel_bias.shape[0] // 2, LANES), I32),
        ),
        in_specs=[VMEM] * 3,
        out_specs=(VMEM,) * 4,
        compiler_params=pltpu.CompilerParams(vmem_limit_bytes=VMEM_LIMIT),
        cost_estimate=pl.CostEstimate(
            flops=4 * COST[0] * rows * width * width, bytes_accessed=0, transcendentals=0
        ),
    )(own, w_proj, rel_bias)

    tick_shape = jax.ShapeDtypeStruct((8, LANES), F32)
    params = pltpu.CompilerParams(vmem_limit_bytes=VMEM_LIMIT)

    def attend(step, blocks, total, *more, weight, given=False, tell=True):
        flops = weight * 2 * rows * width * (width + rows)
        args = [queries, stamp_rows, *blocks, w_proj, table]
        args += [] if total is None else [total]
        args += more
        return pl.pallas_call(
            own_kernel
            if total is None
            else functools.partial(attend_kernel, near, step, given, tell),
            out_shape=(jax.ShapeDtypeStruct((rows, width), F32), tick_shape)[: 1 + tell],
            in_specs=[VMEM] * len(args),
            out_specs=(VMEM, VMEM)[: 1 + tell],
            compiler_params=params,
            cost_estimate=pl.CostEstimate(
                flops=flops, bytes_accessed=0, transcendentals=0
            ),
        )(*args)

    total, tick = attend(0, [own, by_core], None, weight=COST[1])
    began = tick
    by_y = pin(by_y, tick)
    by_both = swap(by_y, 1)
    (total,) = attend(0, [by_y, by_both], total, weight=COST[2], tell=False)
    across = {}
    for step in sorted(far):
        block = pin(far[step], began) if step == levels - 2 else far[step]
        across[step] = swap(block, 2)
        far[step] = [block, swap(block, 1)]
    returned, tick = pl.pallas_call(
        functools.partial(return_kernel, near),
        out_shape=(jax.ShapeDtypeStruct((rows, width), BF16), tick_shape),
        in_specs=[VMEM] * (near + 3),
        out_specs=(VMEM, VMEM),
        scratch_shapes=[pltpu.VMEM((rows, width), BF16), pltpu.VMEM((rows, LANES), I32)],
        compiler_params=params,
        cost_estimate=pl.CostEstimate(
            flops=COST[3] * rows * width * (width + rows), bytes_accessed=0, transcendentals=0
        ),
    )(far[levels - 2][0], own, by_core, by_y, by_both, w_proj, table)
    given = hop(returned, [(0, levels - 1)])
    steps = sorted(far)
    for step in steps:
        extra = (given,) if step == steps[-1] else (tick,)
        total, done = attend(
            step, far[step], total, *extra, weight=COST[4], given=step == steps[-1]
        )
        tick = done if step == steps[0] else tick
    sets = {}
    for step in steps:
        block = pin(across[step], tick)
        sets[step] = [block, swap(block, 1)]
    for step in steps[:-2]:
        (total,) = attend(step, sets[step], total, weight=COST[5], tell=False)
    blocks = [block for step in steps[-2:] for block in sets[step]]
    args = [queries, stamp_rows, *blocks, w_proj, table, total, gate]
    args += [attn_gain.reshape(1, width), w_out, tokens]
    return pl.pallas_call(
        functools.partial(last_kernel, near, steps[-2:]),
        out_shape=jax.ShapeDtypeStruct((rows, width), BF16),
        in_specs=[VMEM] * len(args),
        out_specs=VMEM,
        scratch_shapes=[pltpu.VMEM((rows, width), F32)],
        compiler_params=params,
    )(*args)


def solution(mesh):
    return jax.shard_map(
        functools.partial(body, mesh.shape["pb"]),
        mesh=mesh,
        in_specs=(P(("groups", "pb"), None), P(("groups", "pb")), P(), P(), P(), P(), P()),
        out_specs=P(("groups", "pb"), None),
        check_vma=False,
    )
```

```python
import functools

import jax
import jax.numpy as jnp
from jax import lax
from jax.experimental import pallas as pl
from jax.experimental.pallas import tpu as pltpu
from jax.sharding import PartitionSpec as P

HEADS = 8
BUCKETS = 16
EPSILON = 1e-05
LANES = 128
TAIL = 16
COST = (4, 16, 16, 32, 0, 32, 100)
FIXED = 15
BF16 = jnp.bfloat16
F32 = jnp.float32
I32 = jnp.int32
VMEM = pl.BlockSpec(memory_space=pltpu.VMEM)
SMEM = pl.BlockSpec(memory_space=pltpu.SMEM)
HBM = pl.BlockSpec(memory_space=pltpu.HBM)
VMEM_LIMIT = 12 << 20


def layer_norm(values, gain):
    centered = values - jnp.mean(values, axis=-1, keepdims=True)
    spread = jnp.mean(centered * centered, axis=-1, keepdims=True)
    return centered * lax.rsqrt(spread + EPSILON) * gain


def norm_kernel(tokens_hbm, stamps_hbm, gain_hbm, out_ref, tokens_ref, stamps_ref, gain_ref, sems):
    copies = [
        pltpu.make_async_copy(src, dst, sems.at[i])
        for i, (src, dst) in enumerate(
            ((tokens_hbm, tokens_ref), (stamps_hbm, stamps_ref), (gain_hbm, gain_ref))
        )
    ]
    for copy in copies:
        copy.start()
    for copy in copies:
        copy.wait()
    rows, width = tokens_ref.shape
    out_ref[:rows, :] = layer_norm(tokens_ref[...].astype(F32), gain_ref[...]).astype(BF16)
    stamps = jnp.broadcast_to(stamps_ref[...], (TAIL, rows))
    byte = lax.broadcasted_iota(I32, (TAIL, rows), 0)
    part = jnp.where(byte < 4, lax.shift_right_logical(stamps, 8 * jnp.minimum(byte, 3)) & 255, 0)
    out_ref[rows:, :] = jnp.zeros((TAIL, width), BF16)
    out_ref[rows:, :rows] = part.astype(F32).astype(BF16)


def stamps_of(block):
    rows = block.shape[0] - TAIL
    part = block[rows:, :rows].astype(F32).astype(I32)
    return part[0:1] + part[1:2] * 256 + part[2:3] * 65536 + part[3:4] * 16777216


def down_rows(stamps):
    rows = stamps.shape[1]
    pad = -rows % LANES
    stamps = jnp.concatenate([stamps, jnp.zeros((1, pad), I32)], axis=1)
    return jnp.broadcast_to(stamps, (LANES, rows + pad)).T[:rows, :]


def queries_of(normed, weight):
    width = normed.shape[1]
    scale = 0.5 * (width // HEADS) ** -0.5
    queries = jnp.dot(normed, weight, preferred_element_type=F32)
    return (queries.astype(BF16).astype(F32) * scale).astype(BF16)


def relay_kernel(own_ref, other_ref, out_ref):
    del other_ref
    out_ref[...] = own_ref[...]


def front_kernel(own_ref, w_ref, bias_ref, tokens_ref, wo_ref, gain_ref, *refs):
    q_ref, gate_ref, stamp_ref, table_ref, tokens_out, wo_out, gain_out = refs
    gain_out[...] = gain_ref[...]
    tokens_out[...] = tokens_ref[...]
    wo_out[...] = wo_ref[...]
    rows, width = q_ref.shape
    stamp_ref[...] = down_rows(stamps_of(own_ref))
    normed = own_ref[:rows, :]
    gate = jnp.dot(normed, w_ref[:, :width], preferred_element_type=F32)
    gate_ref[...] = (gate / (1 + jnp.exp(-gate))).astype(BF16)
    q_ref[...] = queries_of(normed, w_ref[:, width : 2 * width])
    heads, buckets = bias_ref.shape
    bias = jnp.concatenate([bias_ref[...], jnp.zeros((heads, LANES - buckets), F32)], axis=1)
    lane = lax.broadcasted_iota(I32, (heads, LANES), 1)
    bucket = jnp.clip(lax.shift_right_logical(33 - jnp.minimum(lane, 32), 1), 0, buckets - 1)
    half = 0.5 * jnp.take_along_axis(bias, bucket, axis=1)
    for p in range(heads // 2):
        low = jnp.floor(half[2 * p + 1 : 2 * p + 2] * 2.0**FIXED + 0.5)
        high = jnp.floor(half[2 * p : 2 * p + 1] * 2.0**FIXED - low * 2.0**-16 + 0.5)
        table_ref[p : p + 1, :] = high.astype(I32) * 65536 + low.astype(I32)


def add_blocks(q_ref, stamp_ref, blocks, w_ref, table_ref, acc_ref, out_ref, hide=None):
    rows, width = q_ref.shape
    size = width // HEADS
    keys = len(blocks) * rows
    normed = jnp.concatenate([b[:rows, :] for b in blocks], axis=0)
    key_rows = jnp.dot(
        normed, w_ref[:, 2 * width : 3 * width], preferred_element_type=F32
    ).astype(BF16)
    value_rows = jnp.dot(normed, w_ref[:, 3 * width :], preferred_element_type=F32).astype(BF16)
    stamps = jnp.concatenate([stamps_of(b) for b in blocks], axis=1)
    cuts = [slice(j * LANES, (j + 1) * LANES) for j in range(keys // LANES)]
    index = [lax.clz(stamp_ref[...] - stamps[:, cut]) for cut in cuts]
    head = lax.broadcasted_iota(I32, (1, LANES), 1) // size
    zero = jnp.zeros((), BF16)
    for p in range(HEADS // 2):
        pair = slice(p * LANES, (p + 1) * LANES)
        both = jnp.concatenate(
            [jnp.where(head == h, key_rows[:, pair], zero) for h in (0, 1)], axis=0
        )
        score = lax.dot_general(
            q_ref[:, pair], both, (((1,), (1,)), ((), ())), preferred_element_type=F32
        )
        table = jnp.broadcast_to(table_ref[p : p + 1, :], (rows, LANES))
        words = [jnp.take_along_axis(table, i, axis=1) for i in index]
        weight = []
        for h in (0, 1):
            for j, word in enumerate(words):
                code = lax.shift_left(word, 16) if h else word
                at = h * keys + j * LANES
                half = score[:, at : at + LANES] + code.astype(F32) * 2.0 ** (-16 - FIXED)
                if hide is not None:
                    half = half + hide[j]
                weight.append((half * jnp.tanh(half) + half).astype(BF16))
        values = jnp.concatenate(
            [jnp.where(head == h, value_rows[:, pair], zero) for h in (0, 1)], axis=0
        )
        mixed = jnp.dot(
            jnp.concatenate(weight, axis=1), values, preferred_element_type=F32
        )
        if acc_ref is not None:
            mixed = acc_ref[:, pair] + mixed
        out_ref[:, pair] = mixed.astype(out_ref.dtype)


def place(near):
    me = lax.axis_index("pb")
    return me // near, me % near


def own_kernel(q_ref, stamp_ref, own_ref, other_ref, w_ref, table_ref, out_ref, tick_ref):
    rows = q_ref.shape[0]
    core = lax.axis_index("pb") % 2
    col = lax.broadcasted_iota(I32, (1, 2 * rows), 1)
    key = jnp.where(col < rows, core * rows + col, (1 - core) * rows + col - rows)
    query = core * rows + lax.broadcasted_iota(I32, (rows, LANES), 0)
    hide = [
        jnp.where(key[:, at : at + LANES] <= query, 0.0, -1e30)
        for at in range(0, 2 * rows, LANES)
    ]
    blocks = (own_ref, other_ref)
    add_blocks(q_ref, stamp_ref, blocks, w_ref, table_ref, None, out_ref, hide)
    tick_ref[...] = jnp.zeros_like(tick_ref)


def attend_kernel(near, step, tell, q_ref, stamp_ref, *refs):
    blocks = refs[:2]
    w_ref, table_ref, acc_ref = refs[2:5]
    out_ref = refs[-2] if tell else refs[-1]
    level, spot = place(near)
    seen = level >= step if step else spot >= near // 2

    @pl.when(seen)
    def _():
        add_blocks(q_ref, stamp_ref, blocks, w_ref, table_ref, acc_ref, out_ref)

    @pl.when(jnp.logical_not(seen))
    def _():
        out_ref[...] = acc_ref[...]

    if tell:
        refs[-1][...] = jnp.zeros_like(refs[-1])


def return_kernel(near, asked_ref, *refs):
    blocks = refs[:near]
    w_ref, table_ref, out_ref, tick_ref, q_ref, stamp_ref = refs[near:]
    tick_ref[...] = jnp.zeros_like(tick_ref)

    @pl.when(place(near)[0] == 0)
    def _():
        rows, width = out_ref.shape
        q_ref[...] = queries_of(asked_ref[:rows, :], w_ref[:, width : 2 * width])
        stamp_ref[...] = down_rows(stamps_of(asked_ref))
        add_blocks(q_ref, stamp_ref, blocks, w_ref, table_ref, None, out_ref)


def last_kernel(near, steps, q_ref, stamp_ref, *refs):
    count = 2 * len(steps)
    blocks = refs[:count]
    w_ref, table_ref, acc_ref, gate_ref, gain_ref, wo_ref, tokens_ref = refs[count:-2]
    out_ref, sum_ref = refs[-2:]
    level = place(near)[0]
    for i in range(len(steps) + 1):
        low = level >= steps[i - 1] if i else True
        high = level < steps[i] if i < len(steps) else True

        @pl.when(jnp.logical_and(low, high))
        def _(i=i):
            if i == 0:
                sum_ref[...] = acc_ref[...]
            else:
                seen = blocks[: 2 * i]
                add_blocks(q_ref, stamp_ref, seen, w_ref, table_ref, acc_ref, sum_ref)

    gated = layer_norm(sum_ref[...], gain_ref[...]) * gate_ref[...].astype(F32)
    mixed = jnp.dot(gated.astype(BF16), wo_ref[...], preferred_element_type=F32)
    out_ref[...] = (tokens_ref[...].astype(F32) + mixed).astype(BF16)


def sum_kernel(sum_ref, more_ref, out_ref):
    out_ref[...] = sum_ref[...] + more_ref[...].astype(F32)


def pin_kernel(block_ref, tick_ref, out_ref):
    del block_ref, tick_ref, out_ref


def pin(block, tick):
    return pl.pallas_call(
        pin_kernel,
        out_shape=jax.ShapeDtypeStruct(block.shape, block.dtype),
        in_specs=[pl.BlockSpec(memory_space=pl.ANY)] * 2,
        out_specs=pl.BlockSpec(memory_space=pl.ANY),
        input_output_aliases={0: 0},
        compiler_params=pltpu.CompilerParams(vmem_limit_bytes=1 << 20),
    )(block, tick)


def body(shards, tokens, stamps, norm_gain, w_proj, rel_bias, attn_gain, w_out):
    rows, width = tokens.shape
    near = 4
    levels = shards // near

    def swap(block, bit):
        return lax.ppermute(block, "pb", [(i, i ^ bit) for i in range(shards)])

    def hop(block, pairs):
        return lax.ppermute(
            block, "pb", [(a * near + i, b * near + i) for a, b in pairs for i in range(near)]
        )

    own = pl.pallas_call(
        norm_kernel,
        out_shape=jax.ShapeDtypeStruct((rows + TAIL, width), BF16),
        in_specs=[HBM] * 3,
        out_specs=VMEM,
        scratch_shapes=[
            pltpu.VMEM((rows, width), BF16),
            pltpu.VMEM((1, rows), I32),
            pltpu.VMEM((1, width), F32),
            pltpu.SemaphoreType.DMA((3,)),
        ],
        compiler_params=pltpu.CompilerParams(vmem_limit_bytes=56 << 20),
    )(tokens, stamps.reshape(1, rows), norm_gain.reshape(1, width))

    far = {}
    for step in range(levels - 2, 0, -1):
        pairs = [(z, z + step) for z in range(levels - step)]
        if step == 1:
            pairs.append((levels - 1, 0))
        far[step] = hop(own, pairs)
    by_core = swap(own, 1)
    own = pl.pallas_call(
        relay_kernel,
        out_shape=jax.ShapeDtypeStruct(own.shape, BF16),
        in_specs=[VMEM] * 2,
        out_specs=VMEM,
        compiler_params=pltpu.CompilerParams(vmem_limit_bytes=2 << 20),
        cost_estimate=pl.CostEstimate(
            flops=COST[6] * rows * width * width, bytes_accessed=0, transcendentals=0
        ),
    )(own, by_core)
    by_y = swap(own, 2)
    queries, gate, stamp_rows, table, tokens, w_out, attn_gain = pl.pallas_call(
        front_kernel,
        out_shape=(
            jax.ShapeDtypeStruct((rows, width), BF16),
            jax.ShapeDtypeStruct((rows, width), BF16),
            jax.ShapeDtypeStruct((rows, LANES), I32),
            jax.ShapeDtypeStruct((rel_bias.shape[0] // 2, LANES), I32),
            jax.ShapeDtypeStruct(tokens.shape, BF16),
            jax.ShapeDtypeStruct(w_out.shape, BF16),
            jax.ShapeDtypeStruct((1, width), F32),
        ),
        in_specs=[VMEM] * 6,
        out_specs=(VMEM,) * 7,
        compiler_params=pltpu.CompilerParams(vmem_limit_bytes=VMEM_LIMIT),
        cost_estimate=pl.CostEstimate(
            flops=4 * COST[0] * rows * width * width, bytes_accessed=0, transcendentals=0
        ),
    )(own, w_proj, rel_bias, tokens, w_out, attn_gain.reshape(1, width))

    tick_shape = jax.ShapeDtypeStruct((8, LANES), F32)
    params = pltpu.CompilerParams(vmem_limit_bytes=VMEM_LIMIT)

    def attend(step, blocks, total, *more, weight, tell=True):
        flops = weight * 2 * rows * width * (width + rows)
        args = [queries, stamp_rows, *blocks, w_proj, table]
        args += [] if total is None else [total]
        args += more
        return pl.pallas_call(
            own_kernel
            if total is None
            else functools.partial(attend_kernel, near, step, tell),
            out_shape=(jax.ShapeDtypeStruct((rows, width), F32), tick_shape)[: 1 + tell],
            in_specs=[VMEM] * len(args),
            out_specs=(VMEM, VMEM)[: 1 + tell],
            compiler_params=params,
            cost_estimate=pl.CostEstimate(
                flops=flops, bytes_accessed=0, transcendentals=0
            ),
        )(*args)

    total, tick = attend(0, [own, by_core], None, weight=COST[1])
    began = tick
    by_y = pin(by_y, tick)
    by_both = swap(by_y, 1)
    (total,) = attend(0, [by_y, by_both], total, weight=COST[2], tell=False)
    across = {}

    def pass_on(step, block):
        across[step] = swap(block, 2)
        far[step] = [block, swap(block, 1)]

    pass_on(1, pin(far[1], began))
    returned, tick = pl.pallas_call(
        functools.partial(return_kernel, near),
        out_shape=(jax.ShapeDtypeStruct((rows, width), BF16), tick_shape),
        in_specs=[VMEM] * (near + 3),
        out_specs=(VMEM, VMEM),
        scratch_shapes=[pltpu.VMEM((rows, width), BF16), pltpu.VMEM((rows, LANES), I32)],
        compiler_params=params,
        cost_estimate=pl.CostEstimate(
            flops=COST[3] * rows * width * (width + rows), bytes_accessed=0, transcendentals=0
        ),
    )(far[1][0], own, by_core, by_y, by_both, w_proj, table)
    given = hop(returned, [(0, levels - 1)])
    steps = sorted(far)
    for step in steps[1:]:
        pass_on(step, far[step])
    for step in steps:
        last = step == steps[-1]
        extra = (tick,) if step == 1 else ()
        total, *told = attend(step, far[step], total, *extra, weight=COST[4], tell=last)
    (tick,) = told
    sets = {}
    for step in steps:
        block = pin(across[step], tick)
        sets[step] = [block, swap(block, 1)]
    for step in steps[:-2]:
        (total,) = attend(step, sets[step], total, weight=COST[5], tell=False)
    total = pl.pallas_call(
        sum_kernel,
        out_shape=jax.ShapeDtypeStruct((rows, width), F32),
        in_specs=[VMEM] * 2,
        out_specs=VMEM,
        compiler_params=pltpu.CompilerParams(vmem_limit_bytes=2 << 20),
        cost_estimate=pl.CostEstimate(
            flops=COST[5] * rows * width * width, bytes_accessed=0, transcendentals=0
        ),
    )(total, given)
    blocks = [block for step in steps[-2:] for block in sets[step]]
    args = [queries, stamp_rows, *blocks, w_proj, table, total, gate]
    args += [attn_gain, w_out, tokens]
    return pl.pallas_call(
        functools.partial(last_kernel, near, steps[-2:]),
        out_shape=jax.ShapeDtypeStruct((rows, width), BF16),
        in_specs=[VMEM] * len(args),
        out_specs=VMEM,
        scratch_shapes=[pltpu.VMEM((rows, width), F32)],
        compiler_params=params,
    )(*args)


def solution(mesh):
    return jax.shard_map(
        functools.partial(body, mesh.shape["pb"]),
        mesh=mesh,
        in_specs=(P(("groups", "pb"), None), P(("groups", "pb")), P(), P(), P(), P(), P()),
        out_specs=P(("groups", "pb"), None),
        check_vma=False,
    )
```

```python
import functools

import jax
import jax.numpy as jnp
from jax import lax
from jax.experimental import pallas as pl
from jax.experimental.pallas import tpu as pltpu
from jax.sharding import PartitionSpec as P

HEADS = 8
BUCKETS = 16
EPSILON = 1e-05
LANES = 128
TAIL = 16
COST = (4, 16, 16, 32, 0, 0, 100)
FIXED = 15
BF16 = jnp.bfloat16
F32 = jnp.float32
I32 = jnp.int32
VMEM = pl.BlockSpec(memory_space=pltpu.VMEM)
SMEM = pl.BlockSpec(memory_space=pltpu.SMEM)
HBM = pl.BlockSpec(memory_space=pltpu.HBM)
VMEM_LIMIT = 12 << 20


def layer_norm(values, gain):
    centered = values - jnp.mean(values, axis=-1, keepdims=True)
    spread = jnp.mean(centered * centered, axis=-1, keepdims=True)
    return centered * lax.rsqrt(spread + EPSILON) * gain


def norm_kernel(tokens_hbm, stamps_hbm, gain_hbm, out_ref, tokens_ref, stamps_ref, gain_ref, sems):
    copies = [
        pltpu.make_async_copy(src, dst, sems.at[i])
        for i, (src, dst) in enumerate(
            ((tokens_hbm, tokens_ref), (stamps_hbm, stamps_ref), (gain_hbm, gain_ref))
        )
    ]
    for copy in copies:
        copy.start()
    for copy in copies:
        copy.wait()
    rows, width = tokens_ref.shape
    out_ref[:rows, :] = layer_norm(tokens_ref[...].astype(F32), gain_ref[...]).astype(BF16)
    stamps = jnp.broadcast_to(stamps_ref[...], (TAIL, rows))
    byte = lax.broadcasted_iota(I32, (TAIL, rows), 0)
    part = jnp.where(byte < 4, lax.shift_right_logical(stamps, 8 * jnp.minimum(byte, 3)) & 255, 0)
    out_ref[rows:, :] = jnp.zeros((TAIL, width), BF16)
    out_ref[rows:, :rows] = part.astype(F32).astype(BF16)


def stamps_of(block):
    rows = block.shape[0] - TAIL
    part = block[rows:, :rows].astype(F32).astype(I32)
    return part[0:1] + part[1:2] * 256 + part[2:3] * 65536 + part[3:4] * 16777216


def down_rows(stamps):
    rows = stamps.shape[1]
    pad = -rows % LANES
    stamps = jnp.concatenate([stamps, jnp.zeros((1, pad), I32)], axis=1)
    return jnp.broadcast_to(stamps, (LANES, rows + pad)).T[:rows, :]


def queries_of(normed, weight):
    width = normed.shape[1]
    scale = 0.5 * (width // HEADS) ** -0.5
    queries = jnp.dot(normed, weight, preferred_element_type=F32)
    return (queries.astype(BF16).astype(F32) * scale).astype(BF16)


def relay_kernel(own_ref, other_ref, out_ref):
    del other_ref
    out_ref[...] = own_ref[...]


def front_kernel(own_ref, w_ref, bias_ref, tokens_ref, wo_ref, gain_ref, *refs):
    q_ref, gate_ref, stamp_ref, table_ref, tokens_out, wo_out, gain_out = refs
    gain_out[...] = gain_ref[...]
    tokens_out[...] = tokens_ref[...]
    wo_out[...] = wo_ref[...]
    rows, width = q_ref.shape
    stamp_ref[...] = down_rows(stamps_of(own_ref))
    normed = own_ref[:rows, :]
    gate = jnp.dot(normed, w_ref[:, :width], preferred_element_type=F32)
    gate_ref[...] = (gate / (1 + jnp.exp(-gate))).astype(BF16)
    q_ref[...] = queries_of(normed, w_ref[:, width : 2 * width])
    heads, buckets = bias_ref.shape
    bias = jnp.concatenate([bias_ref[...], jnp.zeros((heads, LANES - buckets), F32)], axis=1)
    lane = lax.broadcasted_iota(I32, (heads, LANES), 1)
    bucket = jnp.clip(lax.shift_right_logical(33 - jnp.minimum(lane, 32), 1), 0, buckets - 1)
    half = 0.5 * jnp.take_along_axis(bias, bucket, axis=1)
    for p in range(heads // 2):
        low = jnp.floor(half[2 * p + 1 : 2 * p + 2] * 2.0**FIXED + 0.5)
        high = jnp.floor(half[2 * p : 2 * p + 1] * 2.0**FIXED - low * 2.0**-16 + 0.5)
        table_ref[p : p + 1, :] = high.astype(I32) * 65536 + low.astype(I32)


def add_blocks(q_ref, stamp_ref, blocks, w_ref, table_ref, acc_ref, out_ref, hide=None):
    rows, width = q_ref.shape
    size = width // HEADS
    keys = len(blocks) * rows
    normed = jnp.concatenate([b[:rows, :] for b in blocks], axis=0)
    key_rows = jnp.dot(
        normed, w_ref[:, 2 * width : 3 * width], preferred_element_type=F32
    ).astype(BF16)
    value_rows = jnp.dot(normed, w_ref[:, 3 * width :], preferred_element_type=F32).astype(BF16)
    stamps = jnp.concatenate([stamps_of(b) for b in blocks], axis=1)
    cuts = [slice(j * LANES, (j + 1) * LANES) for j in range(keys // LANES)]
    index = [lax.clz(stamp_ref[...] - stamps[:, cut]) for cut in cuts]
    head = lax.broadcasted_iota(I32, (1, LANES), 1) // size
    zero = jnp.zeros((), BF16)
    for p in range(HEADS // 2):
        pair = slice(p * LANES, (p + 1) * LANES)
        both = jnp.concatenate(
            [jnp.where(head == h, key_rows[:, pair], zero) for h in (0, 1)], axis=0
        )
        score = lax.dot_general(
            q_ref[:, pair], both, (((1,), (1,)), ((), ())), preferred_element_type=F32
        )
        table = jnp.broadcast_to(table_ref[p : p + 1, :], (rows, LANES))
        words = [jnp.take_along_axis(table, i, axis=1) for i in index]
        weight = []
        for h in (0, 1):
            for j, word in enumerate(words):
                code = lax.shift_left(word, 16) if h else word
                at = h * keys + j * LANES
                half = score[:, at : at + LANES] + code.astype(F32) * 2.0 ** (-16 - FIXED)
                if hide is not None:
                    half = half + hide[j]
                weight.append((half * jnp.tanh(half) + half).astype(BF16))
        values = jnp.concatenate(
            [jnp.where(head == h, value_rows[:, pair], zero) for h in (0, 1)], axis=0
        )
        mixed = jnp.dot(
            jnp.concatenate(weight, axis=1), values, preferred_element_type=F32
        )
        if acc_ref is not None:
            mixed = acc_ref[:, pair] + mixed
        out_ref[:, pair] = mixed.astype(out_ref.dtype)


def place(near):
    me = lax.axis_index("pb")
    return me // near, me % near


def own_kernel(q_ref, stamp_ref, own_ref, other_ref, w_ref, table_ref, out_ref, tick_ref):
    rows = q_ref.shape[0]
    core = lax.axis_index("pb") % 2
    col = lax.broadcasted_iota(I32, (1, 2 * rows), 1)
    key = jnp.where(col < rows, core * rows + col, (1 - core) * rows + col - rows)
    query = core * rows + lax.broadcasted_iota(I32, (rows, LANES), 0)
    hide = [
        jnp.where(key[:, at : at + LANES] <= query, 0.0, -1e30)
        for at in range(0, 2 * rows, LANES)
    ]
    blocks = (own_ref, other_ref)
    add_blocks(q_ref, stamp_ref, blocks, w_ref, table_ref, None, out_ref, hide)
    tick_ref[...] = jnp.zeros_like(tick_ref)


def attend_kernel(near, step, tell, q_ref, stamp_ref, *refs):
    blocks = refs[:2]
    w_ref, table_ref, acc_ref = refs[2:5]
    out_ref = refs[-2] if tell else refs[-1]
    level, spot = place(near)
    seen = level >= step if step else spot >= near // 2

    @pl.when(seen)
    def _():
        add_blocks(q_ref, stamp_ref, blocks, w_ref, table_ref, acc_ref, out_ref)

    @pl.when(jnp.logical_not(seen))
    def _():
        out_ref[...] = acc_ref[...]

    if tell:
        refs[-1][...] = jnp.zeros_like(refs[-1])


def return_kernel(near, asked_ref, *refs):
    blocks = refs[:near]
    w_ref, table_ref, out_ref, tick_ref, q_ref, stamp_ref = refs[near:]
    tick_ref[...] = jnp.zeros_like(tick_ref)

    @pl.when(place(near)[0] == 0)
    def _():
        rows, width = q_ref.shape
        q_ref[...] = queries_of(asked_ref[:rows, :], w_ref[:, width : 2 * width])
        stamp_ref[...] = down_rows(stamps_of(asked_ref))
        out = out_ref.at[pl.ds(0, rows)]
        add_blocks(q_ref, stamp_ref, blocks, w_ref, table_ref, None, out)
        out_ref[rows:, :] = jnp.zeros((out_ref.shape[0] - rows, width), BF16)


def sets_kernel(near, steps, q_ref, stamp_ref, *refs):
    count = 2 * len(steps)
    blocks = refs[:count]
    w_ref, table_ref, acc_ref, out_ref = refs[count:]
    level = place(near)[0]
    for i in range(len(steps) + 1):
        low = level >= steps[i - 1] if i else True
        high = level < steps[i] if i < len(steps) else True

        @pl.when(jnp.logical_and(low, high))
        def _(i=i):
            if i == 0:
                out_ref[...] = acc_ref[...]
            else:
                seen = blocks[: 2 * i]
                add_blocks(q_ref, stamp_ref, seen, w_ref, table_ref, acc_ref, out_ref)


def last_kernel(sum_ref, more_ref, gate_ref, gain_ref, wo_ref, tokens_ref, out_ref):
    attended = sum_ref[...] + more_ref[: sum_ref.shape[0], :].astype(F32)
    gated = layer_norm(attended, gain_ref[...]) * gate_ref[...].astype(F32)
    mixed = jnp.dot(gated.astype(BF16), wo_ref[...], preferred_element_type=F32)
    out_ref[...] = (tokens_ref[...].astype(F32) + mixed).astype(BF16)


def pin_kernel(block_ref, tick_ref, out_ref):
    del block_ref, tick_ref, out_ref


def pin(block, tick):
    return pl.pallas_call(
        pin_kernel,
        out_shape=jax.ShapeDtypeStruct(block.shape, block.dtype),
        in_specs=[pl.BlockSpec(memory_space=pl.ANY)] * 2,
        out_specs=pl.BlockSpec(memory_space=pl.ANY),
        input_output_aliases={0: 0},
        compiler_params=pltpu.CompilerParams(vmem_limit_bytes=1 << 20),
    )(block, tick)


def body(shards, tokens, stamps, norm_gain, w_proj, rel_bias, attn_gain, w_out):
    rows, width = tokens.shape
    near = 4
    levels = shards // near

    def swap(block, bit):
        return lax.ppermute(block, "pb", [(i, i ^ bit) for i in range(shards)])

    def hop(block, pairs):
        return lax.ppermute(
            block, "pb", [(a * near + i, b * near + i) for a, b in pairs for i in range(near)]
        )

    own = pl.pallas_call(
        norm_kernel,
        out_shape=jax.ShapeDtypeStruct((rows + TAIL, width), BF16),
        in_specs=[HBM] * 3,
        out_specs=VMEM,
        scratch_shapes=[
            pltpu.VMEM((rows, width), BF16),
            pltpu.VMEM((1, rows), I32),
            pltpu.VMEM((1, width), F32),
            pltpu.SemaphoreType.DMA((3,)),
        ],
        compiler_params=pltpu.CompilerParams(vmem_limit_bytes=56 << 20),
    )(tokens, stamps.reshape(1, rows), norm_gain.reshape(1, width))

    far = {}
    for step in range(levels - 2, 0, -1):
        pairs = [(z, z + step) for z in range(levels - step)]
        if step == 1:
            pairs.append((levels - 1, 0))
        far[step] = hop(own, pairs)
    by_core = swap(own, 1)
    own = pl.pallas_call(
        relay_kernel,
        out_shape=jax.ShapeDtypeStruct(own.shape, BF16),
        in_specs=[VMEM] * 2,
        out_specs=VMEM,
        compiler_params=pltpu.CompilerParams(vmem_limit_bytes=2 << 20),
        cost_estimate=pl.CostEstimate(
            flops=COST[6] * rows * width * width, bytes_accessed=0, transcendentals=0
        ),
    )(own, by_core)
    by_y = swap(own, 2)
    queries, gate, stamp_rows, table, tokens, w_out, attn_gain = pl.pallas_call(
        front_kernel,
        out_shape=(
            jax.ShapeDtypeStruct((rows, width), BF16),
            jax.ShapeDtypeStruct((rows, width), BF16),
            jax.ShapeDtypeStruct((rows, LANES), I32),
            jax.ShapeDtypeStruct((rel_bias.shape[0] // 2, LANES), I32),
            jax.ShapeDtypeStruct(tokens.shape, BF16),
            jax.ShapeDtypeStruct(w_out.shape, BF16),
            jax.ShapeDtypeStruct((1, width), F32),
        ),
        in_specs=[VMEM] * 6,
        out_specs=(VMEM,) * 7,
        compiler_params=pltpu.CompilerParams(vmem_limit_bytes=VMEM_LIMIT),
        cost_estimate=pl.CostEstimate(
            flops=4 * COST[0] * rows * width * width, bytes_accessed=0, transcendentals=0
        ),
    )(own, w_proj, rel_bias, tokens, w_out, attn_gain.reshape(1, width))

    tick_shape = jax.ShapeDtypeStruct((8, LANES), F32)
    params = pltpu.CompilerParams(vmem_limit_bytes=VMEM_LIMIT)

    def attend(step, blocks, total, *more, weight, tell=True):
        flops = weight * 2 * rows * width * (width + rows)
        args = [queries, stamp_rows, *blocks, w_proj, table]
        args += [] if total is None else [total]
        args += more
        return pl.pallas_call(
            own_kernel
            if total is None
            else functools.partial(attend_kernel, near, step, tell),
            out_shape=(jax.ShapeDtypeStruct((rows, width), F32), tick_shape)[: 1 + tell],
            in_specs=[VMEM] * len(args),
            out_specs=(VMEM, VMEM)[: 1 + tell],
            compiler_params=params,
            cost_estimate=pl.CostEstimate(
                flops=flops, bytes_accessed=0, transcendentals=0
            ),
        )(*args)

    total, tick = attend(0, [own, by_core], None, weight=COST[1])
    began = tick
    by_y = pin(by_y, tick)
    by_both = swap(by_y, 1)
    (total,) = attend(0, [by_y, by_both], total, weight=COST[2], tell=False)
    across = {}

    def pass_on(step, block):
        across[step] = swap(block, 2)
        far[step] = [block, swap(block, 1)]

    pass_on(1, pin(far[1], began))
    returned, tick = pl.pallas_call(
        functools.partial(return_kernel, near),
        out_shape=(jax.ShapeDtypeStruct((rows + 2 * TAIL, width), BF16), tick_shape),
        in_specs=[VMEM] * (near + 3),
        out_specs=(VMEM, VMEM),
        scratch_shapes=[pltpu.VMEM((rows, width), BF16), pltpu.VMEM((rows, LANES), I32)],
        compiler_params=params,
        cost_estimate=pl.CostEstimate(
            flops=COST[3] * rows * width * (width + rows), bytes_accessed=0, transcendentals=0
        ),
    )(far[1][0], own, by_core, by_y, by_both, w_proj, table)
    given = hop(returned, [(0, levels - 1)])
    steps = sorted(far)
    for step in steps[1:]:
        pass_on(step, far[step])
    for step in steps:
        last = step == steps[-1]
        extra = (tick,) if step == 1 else ()
        total, *told = attend(step, far[step], total, *extra, weight=COST[4], tell=last)
    (tick,) = told
    sets = {}
    for step in steps:
        block = pin(across[step], tick)
        sets[step] = [block, swap(block, 1)]
    for step in steps[:-2]:
        (total,) = attend(step, sets[step], total, weight=COST[5], tell=False)
    blocks = [block for step in steps[-2:] for block in sets[step]]
    args = [queries, stamp_rows, *blocks, w_proj, table, total]
    total = pl.pallas_call(
        functools.partial(sets_kernel, near, steps[-2:]),
        out_shape=jax.ShapeDtypeStruct((rows, width), F32),
        in_specs=[VMEM] * len(args),
        out_specs=VMEM,
        compiler_params=params,
        cost_estimate=pl.CostEstimate(
            flops=COST[5] * rows * width * width, bytes_accessed=0, transcendentals=0
        ),
    )(*args)
    return pl.pallas_call(
        last_kernel,
        out_shape=jax.ShapeDtypeStruct((rows, width), BF16),
        in_specs=[VMEM] * 6,
        out_specs=VMEM,
        compiler_params=params,
    )(total, given, gate, attn_gain, w_out, tokens)


def solution(mesh):
    return jax.shard_map(
        functools.partial(body, mesh.shape["pb"]),
        mesh=mesh,
        in_specs=(P(("groups", "pb"), None), P(("groups", "pb")), P(), P(), P(), P(), P()),
        out_specs=P(("groups", "pb"), None),
        check_vma=False,
    )
```

```python
import functools

import jax
import jax.numpy as jnp
from jax import lax
from jax.experimental import pallas as pl
from jax.experimental.pallas import tpu as pltpu
from jax.sharding import PartitionSpec as P

HEADS = 8
BUCKETS = 16
EPSILON = 1e-05
LANES = 128
TAIL = 16
COST = (4, 16, 16, 32, 0, 0, 100)
FIXED = 15
BF16 = jnp.bfloat16
F32 = jnp.float32
I32 = jnp.int32
VMEM = pl.BlockSpec(memory_space=pltpu.VMEM)
SMEM = pl.BlockSpec(memory_space=pltpu.SMEM)
HBM = pl.BlockSpec(memory_space=pltpu.HBM)
VMEM_LIMIT = 12 << 20


def layer_norm(values, gain):
    centered = values - jnp.mean(values, axis=-1, keepdims=True)
    spread = jnp.mean(centered * centered, axis=-1, keepdims=True)
    return centered * lax.rsqrt(spread + EPSILON) * gain


def norm_kernel(tokens_hbm, stamps_hbm, gain_hbm, out_ref, tokens_ref, stamps_ref, gain_ref, sems):
    copies = [
        pltpu.make_async_copy(src, dst, sems.at[i])
        for i, (src, dst) in enumerate(
            ((tokens_hbm, tokens_ref), (stamps_hbm, stamps_ref), (gain_hbm, gain_ref))
        )
    ]
    for copy in copies:
        copy.start()
    for copy in copies:
        copy.wait()
    rows, width = tokens_ref.shape
    out_ref[:rows, :] = layer_norm(tokens_ref[...].astype(F32), gain_ref[...]).astype(BF16)
    stamps = jnp.broadcast_to(stamps_ref[...], (TAIL, rows))
    byte = lax.broadcasted_iota(I32, (TAIL, rows), 0)
    part = jnp.where(byte < 4, lax.shift_right_logical(stamps, 8 * jnp.minimum(byte, 3)) & 255, 0)
    out_ref[rows:, :] = jnp.zeros((TAIL, width), BF16)
    out_ref[rows:, :rows] = part.astype(F32).astype(BF16)


def stamps_of(block):
    rows = block.shape[0] - TAIL
    part = block[rows:, :rows].astype(F32).astype(I32)
    return part[0:1] + part[1:2] * 256 + part[2:3] * 65536 + part[3:4] * 16777216


def down_rows(stamps):
    rows = stamps.shape[1]
    pad = -rows % LANES
    stamps = jnp.concatenate([stamps, jnp.zeros((1, pad), I32)], axis=1)
    return jnp.broadcast_to(stamps, (LANES, rows + pad)).T[:rows, :]


def queries_of(normed, weight):
    width = normed.shape[1]
    scale = 0.5 * (width // HEADS) ** -0.5
    queries = jnp.dot(normed, weight, preferred_element_type=F32)
    return (queries.astype(BF16).astype(F32) * scale).astype(BF16)


def relay_kernel(own_ref, other_ref, out_ref):
    del other_ref
    out_ref[...] = own_ref[...]


def front_kernel(own_ref, w_ref, bias_ref, tokens_ref, wo_ref, gain_ref, *refs):
    q_ref, gate_ref, stamp_ref, table_ref, tokens_out, wo_out, gain_out = refs
    gain_out[...] = gain_ref[...]
    tokens_out[...] = tokens_ref[...]
    wo_out[...] = wo_ref[...]
    rows, width = q_ref.shape
    stamp_ref[...] = down_rows(stamps_of(own_ref))
    normed = own_ref[:rows, :]
    gate = jnp.dot(normed, w_ref[:, :width], preferred_element_type=F32)
    gate_ref[...] = (gate / (1 + jnp.exp(-gate))).astype(BF16)
    q_ref[...] = queries_of(normed, w_ref[:, width : 2 * width])
    heads, buckets = bias_ref.shape
    bias = jnp.concatenate([bias_ref[...], jnp.zeros((heads, LANES - buckets), F32)], axis=1)
    lane = lax.broadcasted_iota(I32, (heads, LANES), 1)
    bucket = jnp.clip(lax.shift_right_logical(33 - jnp.minimum(lane, 32), 1), 0, buckets - 1)
    half = 0.5 * jnp.take_along_axis(bias, bucket, axis=1)
    for p in range(heads // 2):
        low = jnp.floor(half[2 * p + 1 : 2 * p + 2] * 2.0**FIXED + 0.5)
        high = jnp.floor(half[2 * p : 2 * p + 1] * 2.0**FIXED - low * 2.0**-16 + 0.5)
        table_ref[p : p + 1, :] = high.astype(I32) * 65536 + low.astype(I32)


def add_blocks(q_ref, stamp_ref, blocks, w_ref, table_ref, acc_ref, out_ref, hide=None):
    rows, width = q_ref.shape
    size = width // HEADS
    keys = len(blocks) * rows
    normed = jnp.concatenate([b[:rows, :] for b in blocks], axis=0)
    key_rows = jnp.dot(
        normed, w_ref[:, 2 * width : 3 * width], preferred_element_type=F32
    ).astype(BF16)
    value_rows = jnp.dot(normed, w_ref[:, 3 * width :], preferred_element_type=F32).astype(BF16)
    stamps = jnp.concatenate([stamps_of(b) for b in blocks], axis=1)
    cuts = [slice(j * LANES, (j + 1) * LANES) for j in range(keys // LANES)]
    index = [lax.clz(stamp_ref[...] - stamps[:, cut]) for cut in cuts]
    head = lax.broadcasted_iota(I32, (1, LANES), 1) // size
    zero = jnp.zeros((), BF16)
    for p in range(HEADS // 2):
        pair = slice(p * LANES, (p + 1) * LANES)
        both = jnp.concatenate(
            [jnp.where(head == h, key_rows[:, pair], zero) for h in (0, 1)], axis=0
        )
        score = lax.dot_general(
            q_ref[:, pair], both, (((1,), (1,)), ((), ())), preferred_element_type=F32
        )
        table = jnp.broadcast_to(table_ref[p : p + 1, :], (rows, LANES))
        words = [jnp.take_along_axis(table, i, axis=1) for i in index]
        weight = []
        for h in (0, 1):
            for j, word in enumerate(words):
                code = lax.shift_left(word, 16) if h else word
                at = h * keys + j * LANES
                half = score[:, at : at + LANES] + code.astype(F32) * 2.0 ** (-16 - FIXED)
                if hide is not None:
                    half = half + hide[j]
                weight.append((half * jnp.tanh(half) + half).astype(BF16))
        values = jnp.concatenate(
            [jnp.where(head == h, value_rows[:, pair], zero) for h in (0, 1)], axis=0
        )
        mixed = jnp.dot(
            jnp.concatenate(weight, axis=1), values, preferred_element_type=F32
        )
        if acc_ref is not None:
            mixed = acc_ref[:, pair] + mixed
        out_ref[:, pair] = mixed.astype(out_ref.dtype)


def place(near):
    me = lax.axis_index("pb")
    return me // near, me % near


def own_kernel(q_ref, stamp_ref, own_ref, other_ref, w_ref, table_ref, out_ref, tick_ref):
    rows = q_ref.shape[0]
    core = lax.axis_index("pb") % 2
    col = lax.broadcasted_iota(I32, (1, 2 * rows), 1)
    key = jnp.where(col < rows, core * rows + col, (1 - core) * rows + col - rows)
    query = core * rows + lax.broadcasted_iota(I32, (rows, LANES), 0)
    hide = [
        jnp.where(key[:, at : at + LANES] <= query, 0.0, -1e30)
        for at in range(0, 2 * rows, LANES)
    ]
    blocks = (own_ref, other_ref)
    add_blocks(q_ref, stamp_ref, blocks, w_ref, table_ref, None, out_ref, hide)
    tick_ref[...] = jnp.zeros_like(tick_ref)


def attend_kernel(near, step, tell, q_ref, stamp_ref, *refs):
    blocks = refs[:2]
    w_ref, table_ref, acc_ref = refs[2:5]
    out_ref = refs[-2] if tell else refs[-1]
    level, spot = place(near)
    seen = level >= step if step else spot >= near // 2

    @pl.when(seen)
    def _():
        add_blocks(q_ref, stamp_ref, blocks, w_ref, table_ref, acc_ref, out_ref)

    @pl.when(jnp.logical_not(seen))
    def _():
        out_ref[...] = acc_ref[...]

    if tell:
        refs[-1][...] = jnp.zeros_like(refs[-1])


def return_kernel(near, asked_ref, *refs):
    blocks = refs[:near]
    w_ref, table_ref, out_ref, tick_ref, q_ref, stamp_ref = refs[near:]
    tick_ref[...] = jnp.zeros_like(tick_ref)

    @pl.when(place(near)[0] == 0)
    def _():
        rows, width = q_ref.shape
        q_ref[...] = queries_of(asked_ref[:rows, :], w_ref[:, width : 2 * width])
        stamp_ref[...] = down_rows(stamps_of(asked_ref))
        out = out_ref.at[pl.ds(0, rows)]
        add_blocks(q_ref, stamp_ref, blocks, w_ref, table_ref, None, out)
        out_ref[rows:, :] = jnp.zeros((out_ref.shape[0] - rows, width), BF16)


def sets_kernel(near, steps, q_ref, stamp_ref, *refs):
    count = 2 * len(steps)
    blocks = refs[:count]
    w_ref, table_ref, acc_ref, out_ref = refs[count:]
    level = place(near)[0]
    for i in range(len(steps) + 1):
        low = level >= steps[i - 1] if i else True
        high = level < steps[i] if i < len(steps) else True

        @pl.when(jnp.logical_and(low, high))
        def _(i=i):
            if i == 0:
                out_ref[...] = acc_ref[...]
            else:
                seen = blocks[: 2 * i]
                add_blocks(q_ref, stamp_ref, seen, w_ref, table_ref, acc_ref, out_ref)


def last_kernel(sum_ref, more_ref, gate_ref, gain_ref, wo_ref, tokens_ref, out_ref):
    attended = sum_ref[...] + more_ref[: sum_ref.shape[0], :].astype(F32)
    gated = layer_norm(attended, gain_ref[...]) * gate_ref[...].astype(F32)
    mixed = jnp.dot(gated.astype(BF16), wo_ref[...], preferred_element_type=F32)
    out_ref[...] = (tokens_ref[...].astype(F32) + mixed).astype(BF16)


def pin_kernel(block_ref, tick_ref, out_ref):
    del block_ref, tick_ref, out_ref


def pin(block, tick):
    return pl.pallas_call(
        pin_kernel,
        out_shape=jax.ShapeDtypeStruct(block.shape, block.dtype),
        in_specs=[pl.BlockSpec(memory_space=pl.ANY)] * 2,
        out_specs=pl.BlockSpec(memory_space=pl.ANY),
        input_output_aliases={0: 0},
        compiler_params=pltpu.CompilerParams(vmem_limit_bytes=1 << 20),
    )(block, tick)


def body(shards, tokens, stamps, norm_gain, w_proj, rel_bias, attn_gain, w_out):
    rows, width = tokens.shape
    near = 4
    levels = shards // near

    def swap(block, bit):
        return lax.ppermute(block, "pb", [(i, i ^ bit) for i in range(shards)])

    def hop(block, pairs):
        return lax.ppermute(
            block, "pb", [(a * near + i, b * near + i) for a, b in pairs for i in range(near)]
        )

    own = pl.pallas_call(
        norm_kernel,
        out_shape=jax.ShapeDtypeStruct((rows + TAIL, width), BF16),
        in_specs=[HBM] * 3,
        out_specs=VMEM,
        scratch_shapes=[
            pltpu.VMEM((rows, width), BF16),
            pltpu.VMEM((1, rows), I32),
            pltpu.VMEM((1, width), F32),
            pltpu.SemaphoreType.DMA((3,)),
        ],
        compiler_params=pltpu.CompilerParams(vmem_limit_bytes=56 << 20),
    )(tokens, stamps.reshape(1, rows), norm_gain.reshape(1, width))

    far = {}
    for step in range(levels - 2, 0, -1):
        pairs = [(z, z + step) for z in range(levels - step)]
        if step == 1:
            pairs.append((levels - 1, 0))
        far[step] = hop(own, pairs)
    by_core = swap(own, 1)
    own = pl.pallas_call(
        relay_kernel,
        out_shape=jax.ShapeDtypeStruct(own.shape, BF16),
        in_specs=[VMEM] * 2,
        out_specs=VMEM,
        compiler_params=pltpu.CompilerParams(vmem_limit_bytes=2 << 20),
        cost_estimate=pl.CostEstimate(
            flops=COST[6] * rows * width * width, bytes_accessed=0, transcendentals=0
        ),
    )(own, by_core)
    by_y = swap(own, 2)
    queries, gate, stamp_rows, table, tokens, w_out, attn_gain = pl.pallas_call(
        front_kernel,
        out_shape=(
            jax.ShapeDtypeStruct((rows, width), BF16),
            jax.ShapeDtypeStruct((rows, width), BF16),
            jax.ShapeDtypeStruct((rows, LANES), I32),
            jax.ShapeDtypeStruct((rel_bias.shape[0] // 2, LANES), I32),
            jax.ShapeDtypeStruct(tokens.shape, BF16),
            jax.ShapeDtypeStruct(w_out.shape, BF16),
            jax.ShapeDtypeStruct((1, width), F32),
        ),
        in_specs=[VMEM] * 6,
        out_specs=(VMEM,) * 7,
        compiler_params=pltpu.CompilerParams(vmem_limit_bytes=VMEM_LIMIT),
        cost_estimate=pl.CostEstimate(
            flops=4 * COST[0] * rows * width * width, bytes_accessed=0, transcendentals=0
        ),
    )(own, w_proj, rel_bias, tokens, w_out, attn_gain.reshape(1, width))

    tick_shape = jax.ShapeDtypeStruct((8, LANES), F32)
    params = pltpu.CompilerParams(vmem_limit_bytes=VMEM_LIMIT)

    def attend(step, blocks, total, *more, weight, tell=True):
        flops = weight * 2 * rows * width * (width + rows)
        args = [queries, stamp_rows, *blocks, w_proj, table]
        args += [] if total is None else [total]
        args += more
        return pl.pallas_call(
            own_kernel
            if total is None
            else functools.partial(attend_kernel, near, step, tell),
            out_shape=(jax.ShapeDtypeStruct((rows, width), F32), tick_shape)[: 1 + tell],
            in_specs=[VMEM] * len(args),
            out_specs=(VMEM, VMEM)[: 1 + tell],
            compiler_params=params,
            cost_estimate=pl.CostEstimate(
                flops=flops, bytes_accessed=0, transcendentals=0
            ),
        )(*args)

    total, tick = attend(0, [own, by_core], None, weight=COST[1])
    began = tick
    by_y = pin(by_y, tick)
    by_both = swap(by_y, 1)
    (total,) = attend(0, [by_y, by_both], total, weight=COST[2], tell=False)
    across = {}

    def pass_on(step, block):
        across[step] = swap(block, 2)
        far[step] = [block, swap(block, 1)]

    pass_on(1, pin(far[1], began))
    returned, tick = pl.pallas_call(
        functools.partial(return_kernel, near),
        out_shape=(jax.ShapeDtypeStruct((rows + 2 * TAIL, width), BF16), tick_shape),
        in_specs=[VMEM] * (near + 3),
        out_specs=(VMEM, VMEM),
        scratch_shapes=[pltpu.VMEM((rows, width), BF16), pltpu.VMEM((rows, LANES), I32)],
        compiler_params=params,
        cost_estimate=pl.CostEstimate(
            flops=COST[3] * rows * width * (width + rows), bytes_accessed=0, transcendentals=0
        ),
    )(far[1][0], own, by_core, by_y, by_both, w_proj, table)
    given = hop(returned, [(0, levels - 1)])
    steps = sorted(far)
    for step in steps[1:]:
        pass_on(step, far[step])
    sets = {}
    for step in steps:
        extra = (tick,) if step == 1 else ()
        total, done = attend(step, far[step], total, *extra, weight=COST[4])
        block = pin(across[step], done)
        sets[step] = [block, swap(block, 1)]
    for step in steps[:-1]:
        (total,) = attend(step, sets[step], total, weight=COST[5], tell=False)
    blocks = sets[steps[-1]]
    args = [queries, stamp_rows, *blocks, w_proj, table, total]
    total = pl.pallas_call(
        functools.partial(sets_kernel, near, steps[-1:]),
        out_shape=jax.ShapeDtypeStruct((rows, width), F32),
        in_specs=[VMEM] * len(args),
        out_specs=VMEM,
        compiler_params=params,
        cost_estimate=pl.CostEstimate(
            flops=COST[5] * rows * width * width, bytes_accessed=0, transcendentals=0
        ),
    )(*args)
    return pl.pallas_call(
        last_kernel,
        out_shape=jax.ShapeDtypeStruct((rows, width), BF16),
        in_specs=[VMEM] * 6,
        out_specs=VMEM,
        compiler_params=params,
    )(total, given, gate, attn_gain, w_out, tokens)


def solution(mesh):
    return jax.shard_map(
        functools.partial(body, mesh.shape["pb"]),
        mesh=mesh,
        in_specs=(P(("groups", "pb"), None), P(("groups", "pb")), P(), P(), P(), P(), P()),
        out_specs=P(("groups", "pb"), None),
        check_vma=False,
    )
```
